32 devices in a mesh: ctx: 8 (over y, x, core), exp: 4 (over z).
Axes of the slice: x: 2, y: 2, z: 4, core: 2. Of those that a mesh axis runs over, the one named last changes fastest.
Arguments:
- inputs: bfloat16 [1024, 1024], P('exp', 'ctx'), may hold values from -6 to 6
- conv_taps: float32 [1024, 31], P('exp'), may hold values from -1 to 1
- norm_gain: bfloat16 [1024], P('exp'), may hold values from 0.099609375 to 1.8984375
- routes: int32 [1024, 2], P('ctx'), may hold values from 0 to 7, all different within a row; in each aligned block of 128 rows (0 to 127, 128 to 255, ...) at most 32 rows name the same one
- gate_probs: float32 [1024, 2], P('ctx'), may hold values from 0.1 to 0.9
- w_gate: bfloat16 [8, 1024, 4096], P('ctx', None, 'exp'), may hold values from -0.1875 to 0.1875
- w_up: bfloat16 [8, 1024, 4096], P('ctx', None, 'exp'), may hold values from -0.1875 to 0.1875
- w_down: bfloat16 [8, 4096, 1024], P('ctx', 'exp'), may hold values from -0.09375 to 0.09375
- grad_out: bfloat16 [1024, 1024], P('exp', 'ctx'), may hold values from -6 to 6
Outputs:
- layer_out: bfloat16 [1024, 1024], P('exp', 'ctx')
- grad_inputs: bfloat16 [1024, 1024], P('exp', 'ctx')
- grad_taps: float32 [1024, 31], P('exp')
- grad_gain: float32 [1024], P('exp')
- grad_gates: float32 [1024, 2], P('ctx')
- grad_w_gate: bfloat16 [8, 1024, 4096], P('ctx', None, 'exp')
- grad_w_up: bfloat16 [8, 1024, 4096], P('ctx', None, 'exp')
- grad_w_down: bfloat16 [8, 4096, 1024], P('ctx', 'exp')
The draws below stay inside these ranges and needn't reach their ends.
Inputs may be any that keep to these rules, and one draw needn't show every extreme that they name: `routes`: in each aligned block of 128 rows (the rows of one index of ctx) no expert is named by more than 32 rows, a bound that some block reaches; the two experts of a row differ.
All inputs are finite; a program needn't handle non-finite values.
Results may differ from the reference program's by a relative error of at most 0.025.
Values may be sent and summed in bfloat16 or wider, within the bound.
A program may use at most 64 MiB of HBM per device.

```python
import math
import jax
import jax.numpy as jnp
import numpy as np
from jax import lax

D = 1024
FF = 4096
TAPS = 31
TOK = 128
EXPERTS = 8
SEQ = 1024
CAP = 32


def block_scale(rng, dims, pieces, smallest, high):
    level = 1.0
    for axis_at, parts in pieces:
        draws = jax.random.uniform(jax.random.fold_in(jax.random.fold_in(rng, 6), axis_at), (parts,), jnp.float32, smallest / len(pieces), high / len(pieces))
        level = level * jnp.repeat(jnp.exp(draws), dims[axis_at] // parts).reshape((-1,) + (1,) * (len(dims) - 1 - axis_at))
    return level


def deal_out(stream_key, own, number, rows, count, top, most, skew):
    sequence = jax.random.permutation(stream_key, count)
    heavy_load, usual = portions_of(count, rows * top, most, skew, True), portions_of(count, rows * top, most, skew, False)
    places = jnp.arange(count)

    def named(sizes, turn):
        used = int((sizes > 0).sum())
        fixed = max(1, used // 4)
        shifted = fixed + (places - fixed + turn * (used - fixed)) % max(1, count - fixed)
        return jnp.zeros((count,), jnp.int32).at[sequence[jnp.where(places < fixed, places, shifted)]].set(jnp.asarray(sizes, jnp.int32))

    sizes = jnp.where(number % 4 == 0, named(heavy_load, number // 4), named(usual, number - number // 4 - 1))
    mixed = jax.random.permutation(jax.random.fold_in(own, 3), count)
    donor, sink = mixed[0:count // 2 * 2:2], mixed[1:count // 2 * 2:2]
    room = jnp.minimum(sizes[donor] - 1, most - sizes[sink]) // 2
    room = jnp.where((donor == sequence[0]) | (sink == sequence[0]) | (sizes[sink] == 0), 0, jnp.maximum(room, 0))
    shifted = jax.random.randint(jax.random.fold_in(own, 4), (count // 2,), 0, 1 << 20) % (room + 1)
    sizes = sizes.at[donor].add(-shifted).at[sink].add(shifted)
    items = jnp.searchsorted(jnp.cumsum(sizes), jnp.arange(rows * top), side="right").astype(jnp.int32)
    grid = items.reshape(top, rows).T
    grid = grid[jax.random.permutation(jax.random.fold_in(own, 1), rows)]
    turn = jax.random.randint(jax.random.fold_in(own, 2), (rows, 1), 0, top)
    return jnp.take_along_axis(grid, (jnp.arange(top)[None, :] + turn) % top, axis=1)


def portions_of(amount, total, reach, lean, full):
    weights = [(1 << 20) // math.isqrt(rank ** lean) + 1 for rank in range(1, amount + 1)]
    largest = reach if full else min(reach, max(-(-total // amount), total * weights[0] // sum(weights)))
    least = 1 if total - largest >= amount - 1 else 0
    counts, spare = [largest] + [least] * (amount - 1), total - largest - least * (amount - 1)
    while spare > 0:
        free = [i for i in range(1, amount) if counts[i] < largest] or [i for i in range(1, amount) if counts[i] < reach]
        mass, remaining = sum([weights[i] for i in free]), spare
        for i in free:
            more = min(reach - counts[i], max(1, remaining * weights[i] // mass), spare)
            counts[i] = counts[i] + more
            spare = spare - more
    return np.array(counts)


def scatter_about(rng, shape, scale, limit, shards=(), kind=jnp.bfloat16):
    loudness = block_scale(rng, shape, shards, -0.22, 0.18) if shards else 1.0
    array = jax.random.normal(rng, shape, jnp.float32) * scale * loudness
    return jnp.minimum(jnp.maximum(array, -limit), limit).astype(kind)


def setup_inputs(seed: int = 0) -> dict:
    splits = jax.random.split(jax.random.key(seed), 10)
    inputs = scatter_about(splits[0], (D, SEQ), 1.0, 6.0, ((0, 4), (1, 8)))
    conv_taps = scatter_about(splits[1], (D, TAPS), TAPS ** -0.5, 1.0, ((0, 4),), jnp.float32)
    norm_gain = jnp.clip(1.0 + 0.18 * jax.random.normal(splits[2], (D,), jnp.float32), 0.099609375, 1.8984375).astype(jnp.bfloat16)
    routes_keys = jax.random.split(jax.random.fold_in(splits[3], 1), SEQ // TOK)
    routes_turns = jax.random.permutation(jax.random.fold_in(splits[3], 3), SEQ // TOK)
    routes = jax.vmap(lambda own, number: deal_out(jax.random.fold_in(splits[3], 2), own, number, TOK, EXPERTS, 2, CAP, 2))(routes_keys, routes_turns).reshape((SEQ, 2))
    gate_probs = jnp.clip(0.1 + 0.79999997 * jax.random.uniform(splits[4], (SEQ, 2), jnp.float32) ** block_scale(splits[4], (SEQ, 2), ((0, 8),), -0.2, 0.2), 0.1, 0.9)
    w_gate = scatter_about(splits[5], (EXPERTS, D, FF), D ** -0.5, 0.1875, ((0, 8), (2, 4)))
    w_up = scatter_about(splits[6], (EXPERTS, D, FF), D ** -0.5, 0.1875, ((0, 8), (2, 4)))
    w_down = scatter_about(splits[7], (EXPERTS, FF, D), FF ** -0.5, 0.09375, ((0, 8), (1, 4)))
    grad_out = scatter_about(splits[8], (D, SEQ), 1.0, 6.0, ((0, 4), (1, 8)))
    return dict(inputs=inputs, conv_taps=conv_taps, norm_gain=norm_gain, routes=routes, gate_probs=gate_probs, w_gate=w_gate, w_up=w_up, w_down=w_down, grad_out=grad_out)


EPS = 1e-05

def expert_pass(operands):
    rows_x, rows_dy, weight_gate, weight_up, weight_down = operands
    gate_act = jnp.dot(rows_x, weight_gate, preferred_element_type=jnp.float32)
    up_act = jnp.dot(rows_x, weight_up, preferred_element_type=jnp.float32)
    sigma = jax.nn.sigmoid(gate_act)
    hidden = (gate_act * sigma * up_act).astype(jnp.bfloat16)
    result = jnp.dot(hidden, weight_down, preferred_element_type=jnp.float32)
    d_hidden = jnp.dot(rows_dy, weight_down.T, preferred_element_type=jnp.float32)
    grad_down = jnp.dot(hidden.T, rows_dy, preferred_element_type=jnp.float32).astype(jnp.bfloat16)
    d_gate = (d_hidden * up_act * sigma * (1.0 + gate_act * (1.0 - sigma))).astype(jnp.bfloat16)
    d_up = (d_hidden * gate_act * sigma).astype(jnp.bfloat16)
    grad_gate = jnp.dot(rows_x.T, d_gate, preferred_element_type=jnp.float32).astype(jnp.bfloat16)
    grad_up = jnp.dot(rows_x.T, d_up, preferred_element_type=jnp.float32).astype(jnp.bfloat16)
    d_rows = jnp.dot(d_gate, weight_gate.T, preferred_element_type=jnp.float32) + jnp.dot(d_up, weight_up.T, preferred_element_type=jnp.float32)
    return (result, grad_gate, grad_up, grad_down, d_rows)

def reference(inputs, conv_taps, norm_gain, routes, gate_probs, w_gate, w_up, w_down, grad_out):
    half = TAPS // 2
    x_full = inputs.astype(jnp.float32)
    padded = jnp.concatenate([x_full[:, SEQ - half:], x_full, x_full[:, :half]], axis=1)
    conv = jnp.zeros((D, SEQ), jnp.float32)
    for offset in range(TAPS):
        conv = conv + conv_taps[:, offset:offset + 1] * padded[:, offset:offset + SEQ]
    mixed = (x_full + conv).astype(jnp.bfloat16)
    mixed_f = mixed.astype(jnp.float32)
    scale = lax.rsqrt(lax.optimization_barrier(jnp.mean(mixed_f * mixed_f, axis=0)) + EPS)
    gain_f = norm_gain.astype(jnp.float32)
    normed = (mixed_f * gain_f[:, None] * scale[None, :]).astype(jnp.bfloat16)
    blocks = SEQ // TOK
    flat = routes.reshape(blocks, 2 * TOK).astype(jnp.int32)
    onehot = (flat[:, :, None] == jnp.arange(EXPERTS, dtype=jnp.int32)[None, None, :]).astype(jnp.int32)
    before = jnp.cumsum(onehot, axis=1, dtype=jnp.int32) - onehot
    place = lax.optimization_barrier(jnp.sum(before * onehot, axis=2, dtype=jnp.int32))
    block_ids = jnp.arange(blocks, dtype=jnp.int32)[:, None]
    dest = (flat * (blocks * CAP) + block_ids * CAP + place).reshape(-1).astype(jnp.int32)
    total = EXPERTS * blocks * CAP
    gates = gate_probs.reshape(-1)
    token_rows = jnp.repeat(normed.T, 2, axis=0)
    cot_f = grad_out.astype(jnp.float32)
    cot_rows = jnp.repeat(cot_f.T, 2, axis=0)
    scaled_rows = (cot_rows * gates[:, None]).astype(jnp.bfloat16)
    dispatched = jnp.zeros((total, D), jnp.bfloat16).at[dest].set(token_rows).reshape(EXPERTS, blocks * CAP, D)
    dy_rows = jnp.zeros((total, D), jnp.bfloat16).at[dest].set(scaled_rows).reshape(EXPERTS, blocks * CAP, D)
    result, grad_gate, grad_up, grad_down, d_rows = lax.map(expert_pass, (dispatched, dy_rows, w_gate, w_up, w_down))
    picked = result.reshape(total, D)[dest]
    moe = lax.optimization_barrier(jnp.sum((picked * gates[:, None]).reshape(SEQ, 2, D), axis=1))
    layer_out = (mixed_f + moe.T).astype(jnp.bfloat16)
    grad_gates = lax.optimization_barrier(jnp.sum(picked * cot_rows, axis=1)).reshape(SEQ, 2)
    d_normed = lax.optimization_barrier(jnp.sum(d_rows.reshape(total, D)[dest].reshape(SEQ, 2, D), axis=1)).T
    grad_gain = lax.optimization_barrier(jnp.sum(d_normed * mixed_f * scale[None, :], axis=1))
    dots = lax.optimization_barrier(jnp.sum(d_normed * gain_f[:, None] * mixed_f, axis=0))
    d_mixed = cot_f + gain_f[:, None] * d_normed * scale[None, :] - mixed_f * (dots * scale * scale * scale / D)[None, :]
    grad_padded = jnp.concatenate([d_mixed[:, SEQ - half:], d_mixed, d_mixed[:, :half]], axis=1)
    grad_in = d_mixed
    tap_parts = []
    for offset in range(TAPS):
        grad_in = grad_in + conv_taps[:, offset:offset + 1] * grad_padded[:, 2 * half - offset:2 * half - offset + SEQ]
        tap_parts.append(lax.optimization_barrier(jnp.sum(d_mixed * padded[:, offset:offset + SEQ], axis=1)))
    grad_taps = jnp.stack(tap_parts, axis=1)
    return (layer_out, grad_in.astype(jnp.bfloat16), grad_taps, grad_gain, grad_gates, grad_gate, grad_up, grad_down)
```

```python
import functools
import jax
import jax.numpy as jnp
from jax import lax
from jax.experimental import pallas as pl
from jax.experimental.pallas import tpu as pltpu
from jax.sharding import PartitionSpec as P

EPS = 1e-05
EDGE = 16
MESH = pl.DeviceIdType.MESH
F32, BF16 = jnp.float32, jnp.bfloat16
LAST = (((1,), (1,)), ((), ()))
FIRST = (((0,), (0,)), ((), ()))


def dot(a, b, dims=(((1,), (0,)), ((), ()))):
    return lax.dot_general(a, b, dims, preferred_element_type=F32)


def announce(n, m):
    c, e = lax.axis_index("ctx"), lax.axis_index("exp")
    barrier = pltpu.get_barrier_semaphore()

    def ctx_peer(k, _):
        pl.semaphore_signal(barrier, inc=1, device_id=(lax.rem(c + k, n), e), device_id_type=MESH)
        return 0

    def exp_peer(k, _):
        pl.semaphore_signal(barrier, inc=1, device_id=(c, lax.rem(e + k, m)), device_id_type=MESH)
        return 0

    lax.fori_loop(1, n, ctx_peer, 0)
    lax.fori_loop(1, m, exp_peer, 0)
    return barrier


class Exchange:
    def __init__(self, axis, size, src, dst, send, recv):
        self.axis, self.size, self.src, self.dst = axis, size, src, dst
        self.send, self.recv = send, recv
        self.me = lax.axis_index(axis)

    def copy(self, k, slot):
        peer = lax.rem(self.me + k, self.size)
        if self.axis == "ctx":
            where = (peer, lax.axis_index("exp"))
        else:
            where = (lax.axis_index("ctx"), peer)
        slot = peer if slot is None else slot
        return pltpu.make_async_remote_copy(
            src_ref=self.src(peer),
            dst_ref=self.dst(slot),
            send_sem=self.send.at[peer],
            recv_sem=self.recv.at[slot],
            device_id=where,
            device_id_type=MESH,
        )

    def each(self, act):
        def body(k, _):
            act(k)
            return 0

        lax.fori_loop(1, self.size, body, 0)

    def start(self):
        self.each(lambda k: self.copy(k, self.me).start())

    def arrive(self):
        self.each(lambda k: self.copy(k, None).wait_recv())

    def sent(self):
        self.each(lambda k: self.copy(k, self.me).wait_send())


class Halo:
    def __init__(self, n, edges, left, right, sems):
        c, e = lax.axis_index("ctx"), lax.axis_index("exp")
        up, down = lax.rem(c + 1, n), lax.rem(c + n - 1, n)
        make = pltpu.make_async_remote_copy
        self.copies = [
            make(edges.at[1], left, sems.at[0], sems.at[1], device_id=(up, e), device_id_type=MESH),
            make(edges.at[0], right, sems.at[2], sems.at[3], device_id=(down, e), device_id_type=MESH),
        ]

    def start(self):
        for copy in self.copies:
            copy.start()

    def arrive(self):
        for copy in self.copies:
            copy.wait_recv()

    def sent(self):
        for copy in self.copies:
            copy.wait_send()


def column(row):
    return jnp.transpose(jnp.broadcast_to(row, (128, row.shape[1])))


def turn_row(col):
    return jnp.transpose(jnp.broadcast_to(col, (col.shape[0], 128)))[:1]


def windows(block, base, taps):
    rows = block.shape[0]
    for b in range(8):
        offs = [o for o in range(base, base + taps) if o % 8 == b]
        if offs:
            yield b, (block if b == 0 else pltpu.roll(block, rows - b, axis=0)), offs


def layer(n, m, taps, cap, nc,
          x_any, tap_any, gain_any, route_any, prob_any, cot_any, wg_any, wu_any, wd_any,
          lo_ref, gin_ref, tapo_ref, gaino_ref, gateo_ref, gwg_ref, gwu_ref, gwd_ref,
          x_s, tap_s, gain_s, route_s, prob_s, cot_s, wg, wu, wd,
          xp, xs, xe, hl, hr, cots, mx, side, pt, pb, p0s, p1s, gs, gc, sc,
          sdy, sx, rdy, rx, dh, ga, ua, hid, dg, du, sdx, sy, bdx, by,
          zdx, zy, rdx, ry, dots, norm, dmp, de, dl, dr, tp,
          lsem, hs, hs2, *sem):
    me, mine = lax.axis_index("ctx"), lax.axis_index("exp")
    chans, tokens = x_s.shape
    slots = pt.shape[0]
    width, inner = wg.shape
    cw = chans // nc
    it = iter(sem)
    own = pl.ds(pl.multiple_of(me * cap, cap), cap)

    def pair():
        return next(it), next(it)

    def spans(h, k):
        return slice(k * cw, (k + 1) * cw)

    def chan_rows(ref, h, cols=slice(None)):
        if nc == 1:
            return ref[:, cols]
        return jnp.concatenate(
            [ref[k * chans + h * cw : k * chans + (h + 1) * cw, cols] for k in range(m)], axis=0
        )

    def natural(ref, lo, hi):
        if nc == 1:
            return ref[0, :, lo:hi]
        return jnp.concatenate(
            [ref[h, :, spans(h, k)] for k in range(lo // chans, hi // chans) for h in range(nc)], axis=1
        )

    def rows(ref, h):
        return lambda p: ref.at[h, pl.ds(pl.multiple_of(p * cap, cap), cap)]

    def spread(matrix, pieces):
        if cw % 128 == 0:
            full = dot(matrix, jnp.concatenate(pieces, axis=1))
            return [full[:, k * cw : (k + 1) * cw] for k in range(len(pieces))]
        return [dot(matrix, piece) for piece in pieces]

    barrier = announce(n, m)
    loads = [
        pltpu.make_async_copy(src, dst, lsem.at[i])
        for i, (src, dst) in enumerate(
            [(x_any, x_s), (cot_any, cot_s), (route_any, route_s), (prob_any, prob_s),
             (tap_any, tap_s), (gain_any, gain_s)]
        )
    ]
    weights = [
        pltpu.make_async_copy(src.at[0], dst, lsem.at[6 + i])
        for i, (src, dst) in enumerate([(wd_any, wd), (wg_any, wg), (wu_any, wu)])
    ]
    for load in loads:
        load.start()
    for load in weights:
        load.start()
    loads[0].wait()
    loads[1].wait()
    x_t = jnp.transpose(x_s[...].astype(F32))
    xp[EDGE : EDGE + tokens, :] = x_t
    xe[0] = x_t[:EDGE].astype(BF16)
    xe[1] = x_t[tokens - EDGE :].astype(BF16)
    cot_t = jnp.transpose(cot_s[...].astype(F32)).astype(BF16)
    for h in range(nc):
        cots[h, mine] = cot_t[:, h * cw : (h + 1) * cw]
    pl.semaphore_wait(barrier, n + m - 2)

    halo = Halo(n, xe, hl, hr, hs)
    halo.start()
    gather_cot = []
    for h in range(nc):
        gather_cot.append(
            Exchange("exp", m, lambda p, h=h: cots.at[h, mine], lambda s, h=h: cots.at[h, s], *pair())
        )
        gather_cot[h].start()

    for load in loads[2:]:
        load.wait()
    ids = lax.broadcasted_iota(jnp.int32, (n, tokens), 0)
    named = [route_s[k : k + 1, :] for k in range(2)]
    probs = [prob_s[k : k + 1, :] for k in range(2)]
    hot = [(ids == r).astype(F32) for r in named]
    earlier = lax.broadcasted_iota(jnp.int32, (tokens, tokens), 0) < lax.broadcasted_iota(
        jnp.int32, (tokens, tokens), 1
    )
    count = dot((hot[0] + hot[1]).astype(BF16), earlier.astype(F32).astype(BF16))
    place = lax.broadcasted_iota(jnp.int32, (slots, tokens), 0)
    picks = []
    for r, one in zip(named, hot):
        slot = jnp.sum(count * one, axis=0, keepdims=True).astype(jnp.int32)
        picks.append((place == r * cap + slot).astype(F32))
    pt[...] = (picks[0] + picks[1]).astype(BF16)
    gate_slot = jnp.sum(picks[0] * probs[0] + picks[1] * probs[1], axis=1, keepdims=True)
    gs[...] = jnp.broadcast_to(gate_slot, gs.shape)
    turned = [jnp.transpose(p) for p in picks]
    p0s[...] = turned[0].astype(BF16)
    p1s[...] = turned[1].astype(BF16)
    pb[...] = (turned[0] + turned[1]).astype(BF16)
    gc[0] = column(probs[0])
    gc[1] = column(probs[1])
    gain_row = gain_s[...].astype(F32)
    side[mine] = jnp.zeros(side.shape[1:], F32)
    dots[mine] = jnp.zeros(dots.shape[1:], F32)

    halo.arrive()
    xp[:EDGE, :] = hl[...].astype(F32)
    xp[EDGE + tokens :, :] = hr[...].astype(F32)
    base = EDGE - taps // 2
    span = tokens + 24
    squares = jnp.zeros((tokens, 1), F32)
    for h in range(nc):
        lanes = slice(h * cw, (h + 1) * cw)
        block = xp[:, lanes]
        acc = xp[EDGE : EDGE + tokens, lanes]
        for b, moved, offs in windows(block, base, taps):
            xs[b, :, lanes] = moved[:span]
            for o in offs:
                acc = acc + tap_s[o - base : o - base + 1, lanes] * moved[o - b : o - b + tokens]
        mixed = acc.astype(BF16)
        mx[h, mine] = mixed
        mixed = mixed.astype(F32)
        squares = squares + jnp.sum(mixed * mixed, axis=1, keepdims=True)
        side[mine, 1 + h : 2 + h, :cw] = gain_row[:, lanes]
    side[mine, 0:1, :tokens] = turn_row(squares)
    share = Exchange("exp", m, lambda p: side.at[mine], lambda s: side.at[s], *pair())
    share.start()
    gather_x = []
    for h in range(nc):
        gather_x.append(
            Exchange("exp", m, lambda p, h=h: mx.at[h, mine], lambda s, h=h: mx.at[h, s], *pair())
        )
        gather_x[h].start()

    send_dy, send_x = [], []
    for h in range(nc):
        gather_cot[h].arrive()
        for k, part in enumerate(spread(pt[...], [cots[h, k] for k in range(m)])):
            sdy[h, :, spans(h, k)] = (part * gs[:, :cw]).astype(BF16)
        send_dy.append(Exchange("ctx", n, rows(sdy, h), rows(rdy, h), *pair()))
        send_dy[h].start()
        rdy[h, own, :] = sdy[h, own, :]
    share.arrive()
    total = jnp.sum(side[...], axis=0)[:1, :tokens]
    sc[...] = column(lax.rsqrt(total / width + EPS))
    for h in range(nc):
        gather_x[h].arrive()
        normed = [
            (mx[h, k].astype(F32) * side[k, 1 + h : 2 + h, :cw] * sc[:, :cw]).astype(BF16) for k in range(m)
        ]
        for k, part in enumerate(spread(pt[...], normed)):
            sx[h, :, spans(h, k)] = part.astype(BF16)
        send_x.append(Exchange("ctx", n, rows(sx, h), rows(rx, h), *pair()))
        send_x[h].start()
        rx[h, own, :] = sx[h, own, :]

    tile = min(256, inner)
    tiles = [slice(f, f + tile) for f in range(0, inner, tile)]
    weights[0].wait()
    for h in range(nc):
        send_dy[h].arrive()
    d_y = natural(rdy, 0, width)
    for f in tiles:
        dh[:, f] = dot(d_y, wd[f, :], LAST)
    weights[1].wait()
    weights[2].wait()
    for h in range(nc):
        send_x[h].arrive()
        for f in tiles:
            g = dot(rx[h], chan_rows(wg, h, f))
            u = dot(rx[h], chan_rows(wu, h, f))
            ga[:, f] = g if h == 0 else ga[:, f] + g
            ua[:, f] = u if h == 0 else ua[:, f] + u
            if h == nc - 1:
                step = 32
                for r in range(0, slots, step):
                    at = slice(r, r + step)
                    g, u, d = ga[at, f], ua[at, f], dh[at, f]
                    sigma = jax.nn.sigmoid(g)
                    swish = g * sigma
                    hid[at, f] = (swish * u).astype(BF16)
                    dg[at, f] = (d * u * sigma * (1.0 + g * (1.0 - sigma))).astype(BF16)
                    du[at, f] = (d * swish).astype(BF16)

    group = max(1, min(m, 256 // cw))
    send_dx, send_y = [], []
    for h in range(nc):
        for k in range(0, m, group):
            if nc == 1:
                at = slice(k * cw, (k + group) * cw)
                w1, w2 = wg[at, :], wu[at, :]
            else:
                w1, w2 = [
                    jnp.concatenate(
                        [w[j * chans + h * cw : j * chans + (h + 1) * cw, :] for j in range(k, k + group)], axis=0
                    )
                    for w in (wg, wu)
                ]
            part = dot(dg[...], w1, LAST) + dot(du[...], w2, LAST)
            sdx[h, :, k * cw : (k + group) * cw] = part.astype(BF16)
        send_dx.append(Exchange("ctx", n, rows(sdx, h), rows(bdx, h), *pair()))
        send_dx[h].start()
        bdx[h, own, :] = sdx[h, own, :]
    for h in range(nc):
        for k in range(0, m, group):
            if nc == 1:
                w = wd[:, k * cw : (k + group) * cw]
            else:
                w = jnp.concatenate(
                    [wd[:, j * chans + h * cw : j * chans + (h + 1) * cw] for j in range(k, k + group)], axis=1
                )
            sy[h, :, k * cw : (k + group) * cw] = dot(hid[...], w).astype(BF16)
        send_y.append(Exchange("ctx", n, rows(sy, h), rows(by, h), *pair()))
        send_y[h].start()
        by[h, own, :] = sy[h, own, :]

    for f in tiles:
        gwd_ref[f, :] = dot(hid[:, f], natural(rdy, 0, width), FIRST).astype(BF16)
    for lo in range(0, width, 256):
        part = natural(rx, lo, lo + 256)
        gwg_ref[lo : lo + 256, :] = dot(part, dg[...], FIRST).astype(BF16)
        gwu_ref[lo : lo + 256, :] = dot(part, du[...], FIRST).astype(BF16)

    sum_dx, sum_y = [], []
    weighted = jnp.zeros((tokens, cw), F32)
    sum_norm = Exchange("exp", m, lambda p: norm.at[mine], lambda s: norm.at[s], *pair())
    for h in range(nc):
        send_dx[h].arrive()
        full = dot(pb[...], bdx[h])
        for k in range(m):
            part = full[:, spans(h, k)]
            zdx[h, k] = part.astype(BF16)
            weighted = weighted + part * mx[h, k].astype(F32) * side[k, 1 + h : 2 + h, :cw]
        if h == nc - 1:
            row = turn_row(jnp.sum(weighted, axis=1, keepdims=True))
            norm[mine] = jnp.broadcast_to(row, norm.shape[1:])
            sum_norm.start()
        sum_dx.append(
            Exchange("exp", m, lambda p, h=h: zdx.at[h, p], lambda s, h=h: rdx.at[h, s], *pair())
        )
        sum_dx[h].start()
        rdx[h, mine] = zdx[h, mine]

    d0 = jnp.zeros((tokens, cw), F32)
    d1 = jnp.zeros((tokens, cw), F32)

    def combine(h, d0, d1):
        send_y[h].arrive()
        y0, y1 = dot(p0s[...], by[h]), dot(p1s[...], by[h])
        for k in range(m):
            a, b = y0[:, spans(h, k)], y1[:, spans(h, k)]
            zy[h, k] = (a * gc[0, :, :cw] + b * gc[1, :, :cw]).astype(BF16)
            cot = cots[h, k].astype(F32)
            d0, d1 = d0 + a * cot, d1 + b * cot
        sum_y.append(
            Exchange("exp", m, lambda p, h=h: zy.at[h, p], lambda s, h=h: ry.at[h, s], *pair())
        )
        sum_y[h].start()
        ry[h, mine] = zy[h, mine]
        return d0, d1

    for h in range(nc - 1):
        d0, d1 = combine(h, d0, d1)

    for h in range(nc):
        sum_dx[h].arrive()
    sum_norm.arrive()
    q = column(jnp.sum(norm[...], axis=0)[:1])
    scale = sc[...]
    pull = q * scale * scale * scale / width
    for h in range(nc):
        lanes = slice(h * cw, (h + 1) * cw)
        dn = jnp.sum(rdx[h].astype(F32), axis=0)
        mixed = mx[h, mine].astype(F32)
        dm = cots[h, mine].astype(F32) + gain_row[:, lanes] * dn * scale[:, :cw] - mixed * pull[:, :cw]
        dmp[EDGE : EDGE + tokens, lanes] = dm
        de[0, :, lanes] = dm[:EDGE].astype(BF16)
        de[1, :, lanes] = dm[tokens - EDGE :].astype(BF16)
        tp[me, taps : taps + 1, lanes] = jnp.sum(
            dn * mixed * scale[:, :cw], axis=0, keepdims=True
        ).astype(BF16)
    halo_d = Halo(n, de, dl, dr, hs2)
    halo_d.start()
    d0, d1 = combine(nc - 1, d0, d1)
    dots[mine, 0:1, :] = turn_row(jnp.sum(d0, axis=1, keepdims=True))
    dots[mine, 1:2, :] = turn_row(jnp.sum(d1, axis=1, keepdims=True))
    sum_dots = Exchange("exp", m, lambda p: dots.at[mine], lambda s: dots.at[s], *pair())
    sum_dots.start()

    for h in range(nc):
        lanes = slice(h * cw, (h + 1) * cw)
        dm = dmp[EDGE : EDGE + tokens, lanes]
        for j in range(taps):
            o = base + j
            b = o % 8
            term = jnp.sum(dm * xs[b, o - b : o - b + tokens, lanes], axis=0, keepdims=True)
            tp[me, j : j + 1, lanes] = term.astype(BF16)
    sum_taps = Exchange("ctx", n, lambda p: tp.at[me], lambda s: tp.at[s], *pair())
    sum_taps.start()
    halo_d.arrive()
    dmp[:EDGE, :] = dl[...].astype(F32)
    dmp[EDGE + tokens :, :] = dr[...].astype(F32)
    low = EDGE + taps // 2 - (taps - 1)
    for h in range(nc):
        lanes = slice(h * cw, (h + 1) * cw)
        block = dmp[:, lanes]
        acc = dmp[EDGE : EDGE + tokens, lanes]
        for b, moved, offs in windows(block, low, taps):
            for o in offs:
                j = EDGE + taps // 2 - o
                acc = acc + tap_s[j : j + 1, lanes] * moved[o - b : o - b + tokens]
        gin_ref[lanes, :] = jnp.transpose(acc).astype(BF16)
    for h in range(nc):
        sum_y[h].arrive()
        out = mx[h, mine].astype(F32) + jnp.sum(ry[h].astype(F32), axis=0)
        lo_ref[h * cw : (h + 1) * cw, :] = jnp.transpose(out).astype(BF16)
    sum_dots.arrive()
    gateo_ref[...] = jnp.sum(dots[...], axis=0)[:2]
    sum_taps.arrive()
    grads = jnp.sum(tp[...].astype(F32), axis=0)
    tapo_ref[...] = grads[:taps]
    gaino_ref[...] = grads[taps : taps + 1]
    for done in (halo, halo_d, share, sum_norm, sum_dots, sum_taps):
        done.sent()
    for group in (gather_cot, gather_x, send_dy, send_x, send_dx, send_y, sum_dx, sum_y):
        for done in group:
            done.sent()


def finish(*refs):
    count = (len(refs) - 1) // 2
    sem = refs[-1]
    copies = [
        pltpu.make_async_copy(refs[i], refs[count + i], sem.at[i]) for i in range(count)
    ]
    for copy in copies:
        copy.start()
    for copy in copies:
        copy.wait()


def local(inputs, conv_taps, norm_gain, routes, gate_probs, w_gate, w_up, w_down, grad_out):
    chans, tokens = inputs.shape
    taps = conv_taps.shape[1]
    width, inner = w_gate.shape[1:]
    n, m = lax.axis_size("ctx"), lax.axis_size("exp")
    cap = max(tokens // 8, (2 * tokens + n - 1) // n)
    slots = n * cap
    pad = -(-(taps + 1) // 16) * 16
    nc = max(1, chans // 128)
    cw = chans // nc
    vmem = pl.BlockSpec(memory_space=pltpu.VMEM)
    hbm = pl.BlockSpec(memory_space=pl.ANY)
    shape = jax.ShapeDtypeStruct
    dma = pltpu.SemaphoreType.DMA
    V = pltpu.VMEM
    outs = (
        shape((chans, tokens), BF16),
        shape((chans, tokens), BF16),
        shape((taps, chans), F32),
        shape((1, chans), F32),
        shape((2, tokens), F32),
        shape((width, inner), BF16),
        shape((width, inner), BF16),
        shape((inner, width), BF16),
    )
    sizes = [m] * nc + [m] + [m] * nc + [n] * (2 * nc) + [n] * (2 * nc) + [m]
    sizes += [m] * nc + [m] * nc + [m] + [n]
    big = V((nc, slots, m * cw), BF16)
    results = pl.pallas_call(
        functools.partial(layer, n, m, taps, cap, nc),
        out_shape=outs,
        in_specs=[hbm] * 9,
        out_specs=(vmem,) * 8,
        scratch_shapes=[
            V((chans, tokens), BF16), V((taps, chans), F32), V((1, chans), BF16),
            V((2, tokens), jnp.int32), V((2, tokens), F32), V((chans, tokens), BF16),
            V((width, inner), BF16), V((width, inner), BF16), V((inner, width), BF16),
            V((tokens + 2 * EDGE, chans), F32), V((8, tokens + 24, chans), F32),
            V((2, EDGE, chans), BF16), V((EDGE, chans), BF16), V((EDGE, chans), BF16),
            V((nc, m, tokens, cw), BF16), V((nc, m, tokens, cw), BF16),
            V((m, 8, max(tokens, cw)), F32),
            V((slots, tokens), BF16), V((tokens, slots), BF16), V((tokens, slots), BF16),
            V((tokens, slots), BF16),
            V((slots, 128), F32), V((2, tokens, 128), F32), V((tokens, 128), F32),
            big, big, big, big,
            V((slots, inner), F32), V((slots, inner), F32), V((slots, inner), F32),
            V((slots, inner), BF16), V((slots, inner), BF16), V((slots, inner), BF16),
            big, big, big, big,
            V((nc, m, tokens, cw), BF16), V((nc, m, tokens, cw), BF16),
            V((nc, m, tokens, cw), BF16), V((nc, m, tokens, cw), BF16),
            V((m, 8, tokens), F32), V((m, 8, tokens), F32),
            V((tokens + 2 * EDGE, chans), F32),
            V((2, EDGE, chans), BF16), V((EDGE, chans), BF16), V((EDGE, chans), BF16),
            V((n, pad, chans), BF16),
            dma((9,)), dma((4,)), dma((4,)),
            *[dma((s,)) for s in sizes for _ in range(2)],
        ],
        compiler_params=pltpu.CompilerParams(
            collective_id=0, has_side_effects=True, vmem_limit_bytes=48 << 20
        ),
        name="layer",
    )(inputs, conv_taps.T, norm_gain[None], routes.T, gate_probs.T, grad_out, w_gate, w_up, w_down)
    results = pl.pallas_call(
        finish,
        out_shape=outs,
        in_specs=[vmem] * 8,
        out_specs=(hbm,) * 8,
        scratch_shapes=[dma((8,))],
        compiler_params=pltpu.CompilerParams(vmem_limit_bytes=16 << 20),
        name="finish",
    )(*results)
    layer_out, grad_in, grad_taps, grad_gain, grad_gates, grad_gate, grad_up, grad_down = results
    return (
        layer_out,
        grad_in,
        grad_taps.T,
        grad_gain[0],
        grad_gates.T,
        grad_gate[None],
        grad_up[None],
        grad_down[None],
    )


def solution(mesh):
    return jax.shard_map(
        local,
        mesh=mesh,
        in_specs=(
            P("exp", "ctx"),
            P("exp", None),
            P("exp"),
            P("ctx", None),
            P("ctx", None),
            P("ctx", None, "exp"),
            P("ctx", None, "exp"),
            P("ctx", "exp", None),
            P("exp", "ctx"),
        ),
        out_specs=(
            P("exp", "ctx"),
            P("exp", "ctx"),
            P("exp", None),
            P("exp"),
            P("ctx", None),
            P("ctx", None, "exp"),
            P("ctx", None, "exp"),
            P("ctx", "exp", None),
        ),
        check_vma=False,
    )
```

```python
import functools
import jax
import jax.numpy as jnp
from jax import lax
from jax.experimental import pallas as pl
from jax.experimental.pallas import tpu as pltpu
from jax.sharding import PartitionSpec as P

EPS = 1e-05
EDGE = 16
MESH = pl.DeviceIdType.MESH
F32, BF16 = jnp.float32, jnp.bfloat16
LAST = (((1,), (1,)), ((), ()))
FIRST = (((0,), (0,)), ((), ()))


def dot(a, b, dims=(((1,), (0,)), ((), ()))):
    return lax.dot_general(a, b, dims, preferred_element_type=F32)


def announce(n, m):
    c, e = lax.axis_index("ctx"), lax.axis_index("exp")
    barrier = pltpu.get_barrier_semaphore()

    def ctx_peer(k, _):
        pl.semaphore_signal(barrier, inc=1, device_id=(lax.rem(c + k, n), e), device_id_type=MESH)
        return 0

    def exp_peer(k, _):
        pl.semaphore_signal(barrier, inc=1, device_id=(c, lax.rem(e + k, m)), device_id_type=MESH)
        return 0

    lax.fori_loop(1, n, ctx_peer, 0)
    lax.fori_loop(1, m, exp_peer, 0)
    return barrier


class Exchange:
    def __init__(self, axis, size, src, dst, send, recv):
        self.axis, self.size, self.src, self.dst = axis, size, src, dst
        self.send, self.recv = send, recv
        self.me = lax.axis_index(axis)

    def copy(self, k, slot):
        peer = lax.rem(self.me + k, self.size)
        if self.axis == "ctx":
            where = (peer, lax.axis_index("exp"))
        else:
            where = (lax.axis_index("ctx"), peer)
        slot = peer if slot is None else slot
        return pltpu.make_async_remote_copy(
            src_ref=self.src(peer),
            dst_ref=self.dst(slot),
            send_sem=self.send.at[peer],
            recv_sem=self.recv.at[slot],
            device_id=where,
            device_id_type=MESH,
        )

    def each(self, act):
        def body(k, _):
            act(k)
            return 0

        lax.fori_loop(1, self.size, body, 0)

    def start(self):
        self.each(lambda k: self.copy(k, self.me).start())

    def arrive(self):
        self.each(lambda k: self.copy(k, None).wait_recv())

    def sent(self):
        self.each(lambda k: self.copy(k, self.me).wait_send())


class Halo:
    def __init__(self, n, edges, left, right, sems):
        c, e = lax.axis_index("ctx"), lax.axis_index("exp")
        up, down = lax.rem(c + 1, n), lax.rem(c + n - 1, n)
        make = pltpu.make_async_remote_copy
        self.copies = [
            make(edges.at[1], left, sems.at[0], sems.at[1], device_id=(up, e), device_id_type=MESH),
            make(edges.at[0], right, sems.at[2], sems.at[3], device_id=(down, e), device_id_type=MESH),
        ]

    def start(self):
        for copy in self.copies:
            copy.start()

    def arrive(self):
        for copy in self.copies:
            copy.wait_recv()

    def sent(self):
        for copy in self.copies:
            copy.wait_send()


def column(row):
    return jnp.transpose(jnp.broadcast_to(row, (128, row.shape[1])))


def turn_row(col):
    return jnp.transpose(jnp.broadcast_to(col, (col.shape[0], 128)))[:1]


def windows(block, base, taps):
    rows = block.shape[0]
    for b in range(8):
        offs = [o for o in range(base, base + taps) if o % 8 == b]
        if offs:
            yield b, (block if b == 0 else pltpu.roll(block, rows - b, axis=0)), offs


def layer(n, m, taps, cap, nc,
          x_any, tap_any, gain_any, route_any, prob_any, cot_any, wg_any, wu_any, wd_any,
          lo_ref, gin_ref, tapo_ref, gaino_ref, gateo_ref, gwg_ref, gwu_ref, gwd_ref,
          x_s, tap_s, gain_s, route_s, prob_s, cot_s, wg, wu, wd,
          xp, xs, xe, hl, hr, cots, mx, side, pt, pb, p0s, p1s, gs, gc, sc,
          sdy, sx, rdy, rx, sxl, xa, xg, dh, ga, ua, hid, dg, du, sdx, sy, bdx, by, sl, rl, ol, bl,
          zdx, zy, rdx, ry, dots, norm, dmp, de, dl, dr, tp,
          lsem, hs, hs2, *sem):
    me, mine = lax.axis_index("ctx"), lax.axis_index("exp")
    chans, tokens = x_s.shape
    slots = pt.shape[0]
    width, inner = wg.shape
    cw = chans // nc
    it = iter(sem)
    own = pl.ds(pl.multiple_of(me * cap, cap), cap)
    late = nc - 1 if nc > 1 else None
    direct = [h for h in range(nc) if h != late]
    span_all = m * cw

    def pair():
        return next(it), next(it)

    def spans(h, k):
        return slice(k * cw, (k + 1) * cw)

    def chan_rows(ref, h, cols=slice(None)):
        if nc == 1:
            return ref[:, cols]
        return jnp.concatenate(
            [ref[k * chans + h * cw : k * chans + (h + 1) * cw, cols] for k in range(m)], axis=0
        )

    def natural(ref, lo, hi):
        if nc == 1:
            return ref[0, :, lo:hi]
        return jnp.concatenate(
            [ref[h, :, spans(h, k)] for k in range(lo // chans, hi // chans) for h in range(nc)], axis=1
        )

    def rows(ref, *h):
        return lambda p: ref.at[(*h, pl.ds(pl.multiple_of(p * cap, cap), cap))]

    def gain_of(k, h):
        return side[k, 1 + h : 2 + h, :cw]

    def spread(matrix, pieces):
        if cw % 128 == 0:
            full = dot(matrix, jnp.concatenate(pieces, axis=1))
            return [full[:, k * cw : (k + 1) * cw] for k in range(len(pieces))]
        return [dot(matrix, piece) for piece in pieces]

    barrier = announce(n, m)
    loads = [
        pltpu.make_async_copy(src, dst, lsem.at[i])
        for i, (src, dst) in enumerate(
            [(x_any, x_s), (cot_any, cot_s), (route_any, route_s), (prob_any, prob_s),
             (tap_any, tap_s), (gain_any, gain_s)]
        )
    ]
    weights = [
        pltpu.make_async_copy(src.at[0], dst, lsem.at[6 + i])
        for i, (src, dst) in enumerate([(wd_any, wd), (wg_any, wg), (wu_any, wu)])
    ]
    for load in loads:
        load.start()
    for load in weights:
        load.start()
    loads[0].wait()
    loads[1].wait()
    x_t = jnp.transpose(x_s[...].astype(F32))
    xp[EDGE : EDGE + tokens, :] = x_t
    xe[0] = x_t[:EDGE].astype(BF16)
    xe[1] = x_t[tokens - EDGE :].astype(BF16)
    cot_t = jnp.transpose(cot_s[...].astype(F32)).astype(BF16)
    for h in range(nc):
        cots[h, mine] = cot_t[:, h * cw : (h + 1) * cw]
    pl.semaphore_wait(barrier, n + m - 2)

    halo = Halo(n, xe, hl, hr, hs)
    halo.start()
    gather_cot = []
    for h in range(nc):
        gather_cot.append(
            Exchange("exp", m, lambda p, h=h: cots.at[h, mine], lambda s, h=h: cots.at[h, s], *pair())
        )
        gather_cot[h].start()

    for load in loads[2:]:
        load.wait()
    ids = lax.broadcasted_iota(jnp.int32, (n, tokens), 0)
    named = [route_s[k : k + 1, :] for k in range(2)]
    probs = [prob_s[k : k + 1, :] for k in range(2)]
    hot = [(ids == r).astype(F32) for r in named]
    earlier = lax.broadcasted_iota(jnp.int32, (tokens, tokens), 0) < lax.broadcasted_iota(
        jnp.int32, (tokens, tokens), 1
    )
    count = dot((hot[0] + hot[1]).astype(BF16), earlier.astype(F32).astype(BF16))
    place = lax.broadcasted_iota(jnp.int32, (slots, tokens), 0)
    picks = []
    for r, one in zip(named, hot):
        slot = jnp.sum(count * one, axis=0, keepdims=True).astype(jnp.int32)
        picks.append((place == r * cap + slot).astype(F32))
    pt[...] = (picks[0] + picks[1]).astype(BF16)
    gate_slot = jnp.sum(picks[0] * probs[0] + picks[1] * probs[1], axis=1, keepdims=True)
    gs[...] = jnp.broadcast_to(gate_slot, gs.shape)
    turned = [jnp.transpose(p) for p in picks]
    p0s[...] = turned[0].astype(BF16)
    p1s[...] = turned[1].astype(BF16)
    pb[...] = (turned[0] + turned[1]).astype(BF16)
    gc[0] = column(probs[0])
    gc[1] = column(probs[1])
    gain_row = gain_s[...].astype(F32).reshape(1, chans)
    side[mine] = jnp.zeros(side.shape[1:], F32)
    dots[mine] = jnp.zeros(dots.shape[1:], F32)

    halo.arrive()
    xp[:EDGE, :] = hl[...].astype(F32)
    xp[EDGE + tokens :, :] = hr[...].astype(F32)
    base = EDGE - taps // 2
    span = tokens + 24
    squares = jnp.zeros((tokens, 1), F32)
    for h in range(nc):
        lanes = slice(h * cw, (h + 1) * cw)
        block = xp[:, lanes]
        acc = xp[EDGE : EDGE + tokens, lanes]
        for b, moved, offs in windows(block, base, taps):
            xs[b, :, lanes] = moved[:span]
            for o in offs:
                acc = acc + tap_s[o - base : o - base + 1, lanes] * moved[o - b : o - b + tokens]
        mixed = acc.astype(BF16)
        mx[h, mine] = mixed
        mixed = mixed.astype(F32)
        squares = squares + jnp.sum(mixed * mixed, axis=1, keepdims=True)
        side[mine, 1 + h : 2 + h, :cw] = gain_row[:, lanes]
    side[mine, 0:1, :tokens] = turn_row(squares)
    share = Exchange("exp", m, lambda p: side.at[mine], lambda s: side.at[s], *pair())
    share.start()
    if late is not None:
        sxl[...] = dot(pt[...], mx[late, mine]).astype(BF16)
        send_late_x = Exchange("ctx", n, rows(sxl), rows(xg, mine), *pair())
        send_late_x.start()
        xg[mine, own, :] = sxl[own, :]

    if late is not None:
        send_late_x.arrive()
        gather_late = Exchange("exp", m, lambda p: xg.at[mine], lambda s: xg.at[s], *pair())
        gather_late.start()
    for h in range(nc):
        gather_cot[h].arrive()
    gather_mixed = []
    for h in direct:
        gather_mixed.append(
            Exchange("exp", m, lambda p, h=h: mx.at[h, mine], lambda s, h=h: mx.at[h, s], *pair())
        )
        gather_mixed[h].start()
    send_dy = []
    for h in range(nc):
        for k, part in enumerate(spread(pt[...], [cots[h, k] for k in range(m)])):
            sdy[h, :, spans(h, k)] = (part * gs[:, :cw]).astype(BF16)
        send_dy.append(Exchange("ctx", n, rows(sdy, h), rows(rdy, h), *pair()))
        send_dy[h].start()
        rdy[h, own, :] = sdy[h, own, :]
    share.arrive()
    total = jnp.sum(side[...], axis=0)[:1, :tokens]
    sc[...] = column(lax.rsqrt(total / width + EPS))
    send_x = []
    for h in direct:
        gather_mixed[h].arrive()
        for k, part in enumerate(spread(pt[...], [mx[h, k] for k in range(m)])):
            sx[h, :, spans(h, k)] = part.astype(BF16)
        send_x.append(Exchange("ctx", n, rows(sx, h), rows(xa, h), *pair()))
        send_x[h].start()
        xa[h, own, :] = sx[h, own, :]

    tile = min(256, inner)
    tiles = [slice(f, f + tile) for f in range(0, inner, tile)]
    weights[0].wait()
    for h in range(nc):
        send_dy[h].arrive()
    d_y = natural(rdy, 0, width)
    for f in tiles:
        dh[:, f] = dot(d_y, wd[f, :], LAST)
    weights[1].wait()
    weights[2].wait()
    for h in direct:
        send_x[h].arrive()
    if late is not None:
        gather_late.arrive()

    def raw(k, h, at):
        return (xg[k, at, :] if h == late else xa[h, at, spans(h, k)]).astype(F32)

    step = 32
    for r in range(0, slots, step):
        at = slice(r, r + step)
        acc = jnp.zeros((step, cw), F32)
        for k in range(m):
            for h in range(nc):
                acc = acc + raw(k, h, at) * raw(k, h, at)
        unit = lax.rsqrt(jnp.sum(acc, axis=1, keepdims=True) / width + EPS)
        for k in range(m):
            for h in range(nc):
                lo = k * chans + h * cw
                rx[at, lo : lo + cw] = (raw(k, h, at) * gain_of(k, h) * unit).astype(BF16)
    for f in tiles:
        ga[:, f] = dot(rx[...], wg[:, f])
        ua[:, f] = dot(rx[...], wu[:, f])
        for r in range(0, slots, step):
            at = slice(r, r + step)
            g, u, d = ga[at, f], ua[at, f], dh[at, f]
            sigma = jax.nn.sigmoid(g)
            swish = g * sigma
            hid[at, f] = (swish * u).astype(BF16)
            dg[at, f] = (d * u * sigma * (1.0 + g * (1.0 - sigma))).astype(BF16)
            du[at, f] = (d * swish).astype(BF16)

    group = max(1, min(m, 256 // cw))
    def row_grads(h):
        for k in range(0, m, group):
            if nc == 1:
                at = slice(k * cw, (k + group) * cw)
                w1, w2 = wg[at, :], wu[at, :]
            else:
                w1, w2 = [
                    jnp.concatenate(
                        [w[j * chans + h * cw : j * chans + (h + 1) * cw, :] for j in range(k, k + group)], axis=0
                    )
                    for w in (wg, wu)
                ]
            yield k, dot(dg[...], w1, LAST) + dot(du[...], w2, LAST)

    send_dx, send_y = [], []
    if late is not None:
        inner_q = jnp.zeros((slots, cw), F32)
        for k, part in row_grads(late):
            for j in range(k, k + group):
                piece = part[:, (j - k) * cw : (j - k + 1) * cw]
                sl[j] = piece.astype(BF16)
                inner_q = inner_q + piece * xg[j].astype(F32) * gain_of(j, late)
        reduce_late = Exchange("exp", m, lambda p: sl.at[p], lambda s: rl.at[s], *pair())
        reduce_late.start()
        rl[mine] = sl[mine]
        inner_q = jnp.sum(inner_q, axis=1, keepdims=True)
        high = inner_q.astype(BF16).astype(F32)
        lane = lax.broadcasted_iota(jnp.int32, (slots, 128), 1)
        sdx[0, :, span_all:] = jnp.where(
            lane == 0, high, jnp.where(lane == 1, inner_q - high, 0.0)
        ).astype(BF16)
    for h in direct:
        for k, part in row_grads(h):
            sdx[h, :, k * cw : (k + group) * cw] = part.astype(BF16)
        send_dx.append(Exchange("ctx", n, rows(sdx, h), rows(bdx, h), *pair()))
        send_dx[h].start()
        bdx[h, own, :] = sdx[h, own, :]
    for f in tiles:
        gwd_ref[f, :] = dot(hid[:, f], natural(rdy, 0, width), FIRST).astype(BF16)
    for lo in range(0, width, 256):
        part = rx[:, lo : lo + 256]
        gwg_ref[lo : lo + 256, :] = dot(part, dg[...], FIRST).astype(BF16)
        gwu_ref[lo : lo + 256, :] = dot(part, du[...], FIRST).astype(BF16)

    for h in range(nc):
        for k in range(0, m, group):
            if nc == 1:
                w = wd[:, k * cw : (k + group) * cw]
            else:
                w = jnp.concatenate(
                    [wd[:, j * chans + h * cw : j * chans + (h + 1) * cw] for j in range(k, k + group)], axis=1
                )
            sy[h, :, k * cw : (k + group) * cw] = dot(hid[...], w).astype(BF16)
        send_y.append(Exchange("ctx", n, rows(sy, h), rows(by, h), *pair()))
        send_y[h].start()
        by[h, own, :] = sy[h, own, :]

    sum_dx, sum_y = [], []
    weighted = jnp.zeros((tokens, cw), F32)
    sum_norm = Exchange("exp", m, lambda p: norm.at[mine], lambda s: norm.at[s], *pair())
    for h in direct:
        send_dx[h].arrive()
        full = dot(pb[...], bdx[h])
        if h == 0 and late is not None:
            late_q = full[:, span_all : span_all + 1] + full[:, span_all + 1 : span_all + 2]
        for k in range(m):
            part = full[:, spans(h, k)]
            zdx[h, k] = part.astype(BF16)
            weighted = weighted + part * mx[h, k].astype(F32) * gain_of(k, h)
        if h == direct[-1]:
            total_q = jnp.sum(weighted, axis=1, keepdims=True)
            if late is not None:
                total_q = total_q + late_q
            norm[mine] = jnp.broadcast_to(turn_row(total_q), norm.shape[1:])
            sum_norm.start()
        sum_dx.append(
            Exchange("exp", m, lambda p, h=h: zdx.at[h, p], lambda s, h=h: rdx.at[h, s], *pair())
        )
        sum_dx[h].start()
        rdx[h, mine] = zdx[h, mine]
    if late is not None:
        reduce_late.arrive()
        ol[...] = jnp.sum(rl[...].astype(F32), axis=0).astype(BF16)
        send_late = Exchange("ctx", n, rows(ol), rows(bl), *pair())
        send_late.start()
        bl[own, :] = ol[own, :]

    d0 = jnp.zeros((tokens, cw), F32)
    d1 = jnp.zeros((tokens, cw), F32)

    def combine(h, d0, d1):
        send_y[h].arrive()
        y0, y1 = dot(p0s[...], by[h]), dot(p1s[...], by[h])
        for k in range(m):
            a, b = y0[:, spans(h, k)], y1[:, spans(h, k)]
            zy[h, k] = (a * gc[0, :, :cw] + b * gc[1, :, :cw]).astype(BF16)
            cot = cots[h, k].astype(F32)
            d0, d1 = d0 + a * cot, d1 + b * cot
        sum_y.append(
            Exchange("exp", m, lambda p, h=h: zy.at[h, p], lambda s, h=h: ry.at[h, s], *pair())
        )
        sum_y[h].start()
        ry[h, mine] = zy[h, mine]
        return d0, d1

    for h in range(nc):
        d0, d1 = combine(h, d0, d1)
    for h in direct:
        sum_dx[h].arrive()
    sum_norm.arrive()
    if late is not None:
        send_late.arrive()
    q = column(jnp.sum(norm[...], axis=0)[:1])
    scale = sc[...]
    pull = q * scale * scale * scale / width
    for h in range(nc):
        lanes = slice(h * cw, (h + 1) * cw)
        dn = dot(pb[...], bl[...]) if h == late else jnp.sum(rdx[h].astype(F32), axis=0)
        mixed = mx[h, mine].astype(F32)
        dm = cots[h, mine].astype(F32) + gain_row[:, lanes] * dn * scale[:, :cw] - mixed * pull[:, :cw]
        dmp[EDGE : EDGE + tokens, lanes] = dm
        de[0, :, lanes] = dm[:EDGE].astype(BF16)
        de[1, :, lanes] = dm[tokens - EDGE :].astype(BF16)
        tp[me, taps : taps + 1, lanes] = jnp.sum(
            dn * mixed * scale[:, :cw], axis=0, keepdims=True
        ).astype(BF16)
    halo_d = Halo(n, de, dl, dr, hs2)
    halo_d.start()
    for h in range(nc):
        lanes = slice(h * cw, (h + 1) * cw)
        dm = dmp[EDGE : EDGE + tokens, lanes]
        for j in range(taps):
            o = base + j
            b = o % 8
            term = jnp.sum(dm * xs[b, o - b : o - b + tokens, lanes], axis=0, keepdims=True)
            tp[me, j : j + 1, lanes] = term.astype(BF16)
    sum_taps = Exchange("ctx", n, lambda p: tp.at[me], lambda s: tp.at[s], *pair())
    sum_taps.start()
    dots[mine, 0:1, :] = turn_row(jnp.sum(d0, axis=1, keepdims=True))
    dots[mine, 1:2, :] = turn_row(jnp.sum(d1, axis=1, keepdims=True))
    sum_dots = Exchange("exp", m, lambda p: dots.at[mine], lambda s: dots.at[s], *pair())
    sum_dots.start()

    halo_d.arrive()
    dmp[:EDGE, :] = dl[...].astype(F32)
    dmp[EDGE + tokens :, :] = dr[...].astype(F32)
    low = EDGE + taps // 2 - (taps - 1)
    for h in range(nc):
        lanes = slice(h * cw, (h + 1) * cw)
        block = dmp[:, lanes]
        acc = dmp[EDGE : EDGE + tokens, lanes]
        for b, moved, offs in windows(block, low, taps):
            for o in offs:
                j = EDGE + taps // 2 - o
                acc = acc + tap_s[j : j + 1, lanes] * moved[o - b : o - b + tokens]
        gin_ref[lanes, :] = jnp.transpose(acc).astype(BF16)
    for h in range(nc):
        sum_y[h].arrive()
        out = mx[h, mine].astype(F32) + jnp.sum(ry[h].astype(F32), axis=0)
        lo_ref[h * cw : (h + 1) * cw, :] = jnp.transpose(out).astype(BF16)
    sum_dots.arrive()
    gateo_ref[...] = jnp.sum(dots[...], axis=0)[:2]
    sum_taps.arrive()
    grads = jnp.sum(tp[...].astype(F32), axis=0)
    tapo_ref[...] = grads[:taps]
    gaino_ref[...] = grads[taps : taps + 1]
    singles = [halo, halo_d, share, sum_norm, sum_dots, sum_taps]
    if late is not None:
        singles += [reduce_late, send_late, send_late_x, gather_late]
    for group in (singles, gather_cot, gather_mixed, send_x, send_dy, send_dx, send_y, sum_dx, sum_y):
        for done in group:
            done.sent()


def finish(*refs):
    count = (len(refs) - 1) // 2
    sem = refs[-1]
    copies = [
        pltpu.make_async_copy(refs[i], refs[count + i], sem.at[i]) for i in range(count)
    ]
    for copy in copies:
        copy.start()
    for copy in copies:
        copy.wait()


def local(inputs, conv_taps, norm_gain, routes, gate_probs, w_gate, w_up, w_down, grad_out):
    chans, tokens = inputs.shape
    taps = conv_taps.shape[1]
    width, inner = w_gate.shape[1:]
    n, m = lax.axis_size("ctx"), lax.axis_size("exp")
    cap = max(tokens // 8, (2 * tokens + n - 1) // n)
    slots = n * cap
    pad = -(-(taps + 1) // 16) * 16
    nc = max(1, chans // 128)
    cw = chans // nc
    vmem = pl.BlockSpec(memory_space=pltpu.VMEM)
    hbm = pl.BlockSpec(memory_space=pltpu.HBM)
    shape = jax.ShapeDtypeStruct
    dma = pltpu.SemaphoreType.DMA
    V = pltpu.VMEM
    outs = (
        shape((chans, tokens), BF16),
        shape((chans, tokens), BF16),
        shape((taps, chans), F32),
        shape((1, chans), F32),
        shape((2, tokens), F32),
        shape((width, inner), BF16),
        shape((width, inner), BF16),
        shape((inner, width), BF16),
    )
    straight = nc - 1 if nc > 1 else 1
    extra = nc > 1
    sizes = [m] * nc + [m] + [n, m] * extra + [m] * straight + [n] * nc + [n] * straight
    sizes += [m] * extra + [n] * straight + [n] * nc + [m] + [m] * straight + [n] * extra
    sizes += [m] * nc + [n] + [m]
    big = V((nc, slots, m * cw), BF16)
    part = V((straight, slots, m * cw), BF16)
    plus = V((straight, slots, m * cw + 128 * extra), BF16)
    operands = [
        pltpu.with_memory_space_constraint(a, pltpu.HBM)
        for a in (
            inputs, conv_taps.T, norm_gain, routes.T, gate_probs.T, grad_out, w_gate, w_up, w_down
        )
    ]
    results = pl.pallas_call(
        functools.partial(layer, n, m, taps, cap, nc),
        out_shape=outs,
        in_specs=[hbm] * 9,
        out_specs=(vmem,) * 8,
        scratch_shapes=[
            V((chans, tokens), BF16), V((taps, chans), F32), V((chans,), BF16),
            V((2, tokens), jnp.int32), V((2, tokens), F32), V((chans, tokens), BF16),
            V((width, inner), BF16), V((width, inner), BF16), V((inner, width), BF16),
            V((tokens + 2 * EDGE, chans), F32), V((8, tokens + 24, chans), F32),
            V((2, EDGE, chans), BF16), V((EDGE, chans), BF16), V((EDGE, chans), BF16),
            V((nc, m, tokens, cw), BF16), V((nc, m, tokens, cw), BF16),
            V((m, 8, max(tokens, cw)), F32),
            V((slots, tokens), BF16), V((tokens, slots), BF16), V((tokens, slots), BF16),
            V((tokens, slots), BF16),
            V((slots, 128), F32), V((2, tokens, 128), F32), V((tokens, 128), F32),
            big, part, big, V((slots, width), BF16), V((slots, cw), BF16), part, V((m, slots, cw), BF16),
            V((slots, inner), F32), V((slots, inner), F32), V((slots, inner), F32),
            V((slots, inner), BF16), V((slots, inner), BF16), V((slots, inner), BF16),
            plus, big, plus, big,
            V((m, slots, cw), BF16), V((m, slots, cw), BF16), V((slots, cw), BF16), V((slots, cw), BF16),
            V((nc, m, tokens, cw), BF16), V((nc, m, tokens, cw), BF16),
            V((nc, m, tokens, cw), BF16), V((nc, m, tokens, cw), BF16),
            V((m, 8, tokens), F32), V((m, 8, tokens), F32),
            V((tokens + 2 * EDGE, chans), F32),
            V((2, EDGE, chans), BF16), V((EDGE, chans), BF16), V((EDGE, chans), BF16),
            V((n, pad, chans), BF16),
            dma((9,)), dma((4,)), dma((4,)),
            *[dma((s,)) for s in sizes for _ in range(2)],
        ],
        compiler_params=pltpu.CompilerParams(
            collective_id=0, has_side_effects=True, vmem_limit_bytes=36 << 20
        ),
        cost_estimate=pl.CostEstimate(
            flops=18 * slots * width * inner, bytes_accessed=12 * width * inner, transcendentals=slots * inner
        ),
        name="layer",
    )(*operands)
    results = pl.pallas_call(
        finish,
        out_shape=outs,
        in_specs=[vmem] * 8,
        out_specs=(hbm,) * 8,
        scratch_shapes=[dma((8,))],
        compiler_params=pltpu.CompilerParams(vmem_limit_bytes=16 << 20),
        name="finish",
    )(*results)
    layer_out, grad_in, grad_taps, grad_gain, grad_gates, grad_gate, grad_up, grad_down = results
    return (
        layer_out,
        grad_in,
        grad_taps.T,
        grad_gain[0],
        grad_gates.T,
        grad_gate[None],
        grad_up[None],
        grad_down[None],
    )


def solution(mesh):
    return jax.shard_map(
        local,
        mesh=mesh,
        in_specs=(
            P("exp", "ctx"),
            P("exp", None),
            P("exp"),
            P("ctx", None),
            P("ctx", None),
            P("ctx", None, "exp"),
            P("ctx", None, "exp"),
            P("ctx", "exp", None),
            P("exp", "ctx"),
        ),
        out_specs=(
            P("exp", "ctx"),
            P("exp", "ctx"),
            P("exp", None),
            P("exp"),
            P("ctx", None),
            P("ctx", None, "exp"),
            P("ctx", None, "exp"),
            P("ctx", "exp", None),
        ),
        check_vma=False,
    )
```

```python
import functools
import jax
import jax.numpy as jnp
from jax import lax
from jax.experimental import pallas as pl
from jax.experimental.pallas import tpu as pltpu
from jax.sharding import PartitionSpec as P

EPS = 1e-05
EDGE = 16
MESH = pl.DeviceIdType.MESH
F32, BF16 = jnp.float32, jnp.bfloat16
LAST = (((1,), (1,)), ((), ()))
FIRST = (((0,), (0,)), ((), ()))


def dot(a, b, dims=(((1,), (0,)), ((), ()))):
    return lax.dot_general(a, b, dims, preferred_element_type=F32)


def announce(n, m):
    c, e = lax.axis_index("ctx"), lax.axis_index("exp")
    barrier = pltpu.get_barrier_semaphore()

    def ctx_peer(k, _):
        pl.semaphore_signal(barrier, inc=1, device_id=(lax.rem(c + k, n), e), device_id_type=MESH)
        return 0

    def exp_peer(k, _):
        pl.semaphore_signal(barrier, inc=1, device_id=(c, lax.rem(e + k, m)), device_id_type=MESH)
        return 0

    lax.fori_loop(1, n, ctx_peer, 0)
    lax.fori_loop(1, m, exp_peer, 0)
    return barrier


class Exchange:
    def __init__(self, axis, size, src, dst, bulk, send, recv):
        self.axis, self.size, self.src, self.dst = axis, size, src, dst
        self.bulk, self.send, self.recv = bulk, send, recv
        self.me = lax.axis_index(axis)

    def where(self, peer):
        if self.axis == "ctx":
            return peer, lax.axis_index("exp")
        return lax.axis_index("ctx"), peer

    def copy(self, peer, src, dst):
        return pltpu.make_async_remote_copy(
            src_ref=src,
            dst_ref=dst,
            send_sem=self.send,
            recv_sem=self.recv,
            device_id=self.where(peer),
            device_id_type=MESH,
        )

    def start(self):
        def body(k, _):
            peer = lax.rem(self.me + k, self.size)
            self.copy(peer, self.src(peer), self.dst(self.me)).start()
            return 0

        lax.fori_loop(1, self.size, body, 0)

    def all_of_them(self):
        return self.copy(lax.rem(self.me + 1, self.size), self.bulk, self.bulk)

    def arrive(self):
        self.all_of_them().wait_recv()

    def sent(self):
        self.all_of_them().wait_send()


class Halo:
    def __init__(self, n, edges, left, right, sems):
        c, e = lax.axis_index("ctx"), lax.axis_index("exp")
        up, down = lax.rem(c + 1, n), lax.rem(c + n - 1, n)
        make = pltpu.make_async_remote_copy
        self.copies = [
            make(edges.at[1], left, sems.at[0], sems.at[1], device_id=(up, e), device_id_type=MESH),
            make(edges.at[0], right, sems.at[2], sems.at[3], device_id=(down, e), device_id_type=MESH),
        ]

    def start(self):
        for copy in self.copies:
            copy.start()

    def arrive(self):
        for copy in self.copies:
            copy.wait_recv()

    def sent(self):
        for copy in self.copies:
            copy.wait_send()


def column(row):
    return jnp.transpose(jnp.broadcast_to(row, (128, row.shape[1])))


def turn_row(col):
    return jnp.transpose(jnp.broadcast_to(col, (col.shape[0], 128)))[:1]


def windows(block, base, taps):
    rows = block.shape[0]
    for b in range(8):
        offs = [o for o in range(base, base + taps) if o % 8 == b]
        if offs:
            yield b, (block if b == 0 else pltpu.roll(block, rows - b, axis=0)), offs


def layer(n, m, taps, cap, nc,
          x_any, tap_any, gain_any, route_any, prob_any, cot_any, wg_any, wu_any, wd_any,
          lo_ref, gin_ref, tapo_ref, gaino_ref, gateo_ref, gwg_ref, gwu_ref, gwd_ref,
          x_s, tap_s, gain_s, route_s, prob_s, cot_s, wg, wu, wd,
          xp, xs, xe, hl, hr, cots, mx, side, pt, pb, p0s, p1s, gs, gc, sc,
          sdy, sx, rdy, rx, sxl, xa, xg, dh, ga, ua, hid, dg, du, sdx, sy, bdx, by, sl, rl, ol, bl,
          zdx, zy, rdx, ry, dots, norm, dmp, de, dl, dr, tp,
          lsem, hs, hs2, sem):
    me, mine = lax.axis_index("ctx"), lax.axis_index("exp")
    chans, tokens = x_s.shape
    slots = pt.shape[0]
    width, inner = wg.shape
    cw = chans // nc
    it = iter(range(sem.shape[0]))
    own = pl.ds(pl.multiple_of(me * cap, cap), cap)
    most = (n - 1) * cap
    late = nc - 1 if nc > 1 else None
    direct = [h for h in range(nc) if h != late]
    span_all = m * cw

    def pair():
        return sem.at[next(it)], sem.at[next(it)]

    def spans(h, k):
        return slice(k * cw, (k + 1) * cw)

    def natural(ref, lo, hi):
        if nc == 1:
            return ref[0, :, lo:hi]
        return jnp.concatenate(
            [ref[h, :, spans(h, k)] for k in range(lo // chans, hi // chans) for h in range(nc)], axis=1
        )

    def rows(ref, *h):
        return lambda p: ref.at[(*h, pl.ds(pl.multiple_of(p * cap, cap), cap))]

    def gain_of(k, h):
        return side[k, 1 + h : 2 + h, :cw]

    def spread(matrix, pieces):
        if cw % 128 == 0:
            full = dot(matrix, jnp.concatenate(pieces, axis=1))
            return [full[:, k * cw : (k + 1) * cw] for k in range(len(pieces))]
        return [dot(matrix, piece) for piece in pieces]

    barrier = announce(n, m)
    loads = [
        pltpu.make_async_copy(src, dst, lsem.at[i])
        for i, (src, dst) in enumerate(
            [(x_any, x_s), (cot_any, cot_s), (route_any, route_s), (prob_any, prob_s),
             (tap_any, tap_s), (gain_any, gain_s)]
        )
    ]
    weights = [
        pltpu.make_async_copy(src.at[0], dst, lsem.at[6 + i])
        for i, (src, dst) in enumerate([(wd_any, wd), (wg_any, wg), (wu_any, wu)])
    ]
    for load in loads:
        load.start()
    for load in weights:
        load.start()
    loads[0].wait()
    loads[1].wait()
    x_t = jnp.transpose(x_s[...].astype(F32))
    xp[EDGE : EDGE + tokens, :] = x_t
    xe[0] = x_t[:EDGE].astype(BF16)
    xe[1] = x_t[tokens - EDGE :].astype(BF16)
    cot_t = jnp.transpose(cot_s[...].astype(F32)).astype(BF16)
    for h in range(nc):
        cots[h, mine] = cot_t[:, h * cw : (h + 1) * cw]
    pl.semaphore_wait(barrier, n + m - 2)

    halo = Halo(n, xe, hl, hr, hs)
    halo.start()
    gather_cot = []
    for h in range(nc):
        gather_cot.append(
            Exchange("exp", m, lambda p, h=h: cots.at[h, mine], lambda s, h=h: cots.at[h, s], cots.at[h, :m - 1], *pair())
        )
    for h in range(nc):
        gather_cot[h].start()

    for load in loads[2:]:
        load.wait()
    ids = lax.broadcasted_iota(jnp.int32, (n, tokens), 0)
    named = [route_s[k : k + 1, :] for k in range(2)]
    probs = [prob_s[k : k + 1, :] for k in range(2)]
    hot = [(ids == r).astype(F32) for r in named]
    earlier = lax.broadcasted_iota(jnp.int32, (tokens, tokens), 0) < lax.broadcasted_iota(
        jnp.int32, (tokens, tokens), 1
    )
    count = dot((hot[0] + hot[1]).astype(BF16), earlier.astype(F32).astype(BF16))
    place = lax.broadcasted_iota(jnp.int32, (slots, tokens), 0)
    picks = []
    for r, one in zip(named, hot):
        slot = jnp.sum(count * one, axis=0, keepdims=True).astype(jnp.int32)
        picks.append((place == r * cap + slot).astype(F32))
    pt[...] = (picks[0] + picks[1]).astype(BF16)
    gate_slot = jnp.sum(picks[0] * probs[0] + picks[1] * probs[1], axis=1, keepdims=True)
    gs[...] = jnp.broadcast_to(gate_slot, gs.shape)
    turned = [jnp.transpose(p) for p in picks]
    p0s[...] = turned[0].astype(BF16)
    p1s[...] = turned[1].astype(BF16)
    pb[...] = (turned[0] + turned[1]).astype(BF16)
    gc[0] = column(probs[0])
    gc[1] = column(probs[1])
    gain_row = gain_s[...].astype(F32).reshape(1, chans)
    side[mine] = jnp.zeros(side.shape[1:], F32)
    dots[mine] = jnp.zeros(dots.shape[1:], F32)

    halo.arrive()
    xp[:EDGE, :] = hl[...].astype(F32)
    xp[EDGE + tokens :, :] = hr[...].astype(F32)
    base = EDGE - taps // 2
    span = tokens + 24
    squares = jnp.zeros((tokens, 1), F32)
    for h in range(nc):
        lanes = slice(h * cw, (h + 1) * cw)
        block = xp[:, lanes]
        acc = xp[EDGE : EDGE + tokens, lanes]
        for b, moved, offs in windows(block, base, taps):
            xs[b, :, lanes] = moved[:span]
            for o in offs:
                acc = acc + tap_s[o - base : o - base + 1, lanes] * moved[o - b : o - b + tokens]
        mixed = acc.astype(BF16)
        mx[h, mine] = mixed
        mixed = mixed.astype(F32)
        squares = squares + jnp.sum(mixed * mixed, axis=1, keepdims=True)
        side[mine, 1 + h : 2 + h, :cw] = gain_row[:, lanes]
    side[mine, 0:1, :tokens] = turn_row(squares)
    share = Exchange("exp", m, lambda p: side.at[mine], lambda s: side.at[s], side.at[:m - 1], *pair())
    share.start()
    if late is not None:
        sxl[...] = dot(pt[...], mx[late, mine]).astype(BF16)
        launch_x = Exchange("ctx", n, rows(sxl), rows(xg, mine), xg.at[mine, :most], *pair())
        launch_x.start()
        xg[mine, own, :] = sxl[own, :]

    gather_mixed = []
    for h in direct:
        gather_mixed.append(
            Exchange("exp", m, lambda p, h=h: mx.at[h, mine], lambda s, h=h: mx.at[h, s], mx.at[h, :m - 1], *pair())
        )
        gather_mixed[h].start()

    send_dy = []

    def dispatch_cot(h):
        gather_cot[h].arrive()
        for k, part in enumerate(spread(pt[...], [cots[h, k] for k in range(m)])):
            sdy[h, :, spans(h, k)] = (part * gs[:, :cw]).astype(BF16)
        send_dy.append(Exchange("ctx", n, rows(sdy, h), rows(rdy, h), rdy.at[h, :most], *pair()))
        send_dy[h].start()
        rdy[h, own, :] = sdy[h, own, :]

    if late is not None:
        gather_late = Exchange("exp", m, lambda p: xg.at[mine], lambda s: xg.at[s], xg.at[:m - 1], *pair())
    dispatch_cot(0)
    if late is not None:
        launch_x.arrive()
        gather_late.start()
    for h in range(1, nc):
        dispatch_cot(h)
    share.arrive()
    total = jnp.sum(side[...], axis=0)[:1, :tokens]
    sc[...] = column(lax.rsqrt(total / width + EPS))
    send_x = []
    for h in direct:
        gather_mixed[h].arrive()
        for k, part in enumerate(spread(pt[...], [mx[h, k] for k in range(m)])):
            sx[h, :, spans(h, k)] = part.astype(BF16)
        send_x.append(Exchange("ctx", n, rows(sx, h), rows(xa, h), xa.at[h, :most], *pair()))
        send_x[h].start()
        xa[h, own, :] = sx[h, own, :]

    tile = min(256, inner)
    tiles = [slice(f, f + tile) for f in range(0, inner, tile)]
    weights[0].wait()
    for h in range(nc):
        send_dy[h].arrive()
    d_y = natural(rdy, 0, width)
    for f in tiles:
        dh[:, f] = dot(d_y, wd[f, :], LAST)
    weights[1].wait()
    weights[2].wait()
    for h in direct:
        send_x[h].arrive()
    if late is not None:
        gather_late.arrive()

    def raw(k, h, at):
        return (xg[k, at, :] if h == late else xa[h, at, spans(h, k)]).astype(F32)

    step = 32
    for r in range(0, slots, step):
        at = slice(r, r + step)
        acc = jnp.zeros((step, cw), F32)
        for k in range(m):
            for h in range(nc):
                acc = acc + raw(k, h, at) * raw(k, h, at)
        unit = lax.rsqrt(jnp.sum(acc, axis=1, keepdims=True) / width + EPS)
        for k in range(m):
            for h in range(nc):
                lo = k * chans + h * cw
                rx[at, lo : lo + cw] = (raw(k, h, at) * gain_of(k, h) * unit).astype(BF16)
    for f in tiles:
        ga[:, f] = dot(rx[...], wg[:, f])
        ua[:, f] = dot(rx[...], wu[:, f])
        for r in range(0, slots, step):
            at = slice(r, r + step)
            g, u, d = ga[at, f], ua[at, f], dh[at, f]
            sigma = jax.nn.sigmoid(g)
            swish = g * sigma
            hid[at, f] = (swish * u).astype(BF16)
            dg[at, f] = (d * u * sigma * (1.0 + g * (1.0 - sigma))).astype(BF16)
            du[at, f] = (d * swish).astype(BF16)

    group = max(1, min(m, 256 // cw))
    def row_grads(h):
        for k in range(0, m, group):
            if nc == 1:
                at = slice(k * cw, (k + group) * cw)
                w1, w2 = wg[at, :], wu[at, :]
            else:
                w1, w2 = [
                    jnp.concatenate(
                        [w[j * chans + h * cw : j * chans + (h + 1) * cw, :] for j in range(k, k + group)], axis=0
                    )
                    for w in (wg, wu)
                ]
            yield k, dot(dg[...], w1, LAST) + dot(du[...], w2, LAST)

    send_dx, send_y = [], []
    if late is not None:
        inner_q = jnp.zeros((slots, cw), F32)
        for k, part in row_grads(late):
            for j in range(k, k + group):
                piece = part[:, (j - k) * cw : (j - k + 1) * cw]
                sl[j] = piece.astype(BF16)
                inner_q = inner_q + piece * raw(j, late, slice(None)) * gain_of(j, late)
        reduce_late = Exchange("exp", m, lambda p: sl.at[p], lambda s: rl.at[s], rl.at[:m - 1], *pair())
        reduce_late.start()
        rl[mine] = sl[mine]
        inner_q = jnp.sum(inner_q, axis=1, keepdims=True)
        high = inner_q.astype(BF16).astype(F32)
        lane = lax.broadcasted_iota(jnp.int32, (slots, 128), 1)
        sdx[0, :, span_all:] = jnp.where(
            lane == 0, high, jnp.where(lane == 1, inner_q - high, 0.0)
        ).astype(BF16)
    for h in direct:
        for k, part in row_grads(h):
            sdx[h, :, k * cw : (k + group) * cw] = part.astype(BF16)
        send_dx.append(Exchange("ctx", n, rows(sdx, h), rows(bdx, h), bdx.at[h, :most], *pair()))
        send_dx[h].start()
        bdx[h, own, :] = sdx[h, own, :]
    for h in range(nc):
        for k in range(0, m, group):
            if nc == 1:
                w = wd[:, k * cw : (k + group) * cw]
            else:
                w = jnp.concatenate(
                    [wd[:, j * chans + h * cw : j * chans + (h + 1) * cw] for j in range(k, k + group)], axis=1
                )
            sy[h, :, k * cw : (k + group) * cw] = dot(hid[...], w).astype(BF16)
        send_y.append(Exchange("ctx", n, rows(sy, h), rows(by, h), by.at[h, :most], *pair()))
        send_y[h].start()
        by[h, own, :] = sy[h, own, :]

    for f in tiles:
        gwd_ref[f, :] = dot(hid[:, f], natural(rdy, 0, width), FIRST).astype(BF16)
    for lo in range(0, width, 256):
        part = rx[:, lo : lo + 256]
        gwg_ref[lo : lo + 256, :] = dot(part, dg[...], FIRST).astype(BF16)
        gwu_ref[lo : lo + 256, :] = dot(part, du[...], FIRST).astype(BF16)

    sum_dx, sum_y = [], []
    weighted = jnp.zeros((tokens, cw), F32)
    sum_norm = Exchange("exp", m, lambda p: norm.at[mine], lambda s: norm.at[s], norm.at[:m - 1], *pair())
    for h in direct:
        send_dx[h].arrive()
        full = dot(pb[...], bdx[h])
        if h == 0 and late is not None:
            late_q = full[:, span_all : span_all + 1] + full[:, span_all + 1 : span_all + 2]
        for k in range(m):
            part = full[:, spans(h, k)]
            zdx[h, k] = part.astype(BF16)
            weighted = weighted + part * mx[h, k].astype(F32) * gain_of(k, h)
        if h == direct[-1]:
            total_q = jnp.sum(weighted, axis=1, keepdims=True)
            if late is not None:
                total_q = total_q + late_q
            norm[mine] = jnp.broadcast_to(turn_row(total_q), norm.shape[1:])
            sum_norm.start()
        sum_dx.append(
            Exchange("exp", m, lambda p, h=h: zdx.at[h, p], lambda s, h=h: rdx.at[h, s], rdx.at[h, :m - 1], *pair())
        )
        sum_dx[h].start()
        rdx[h, mine] = zdx[h, mine]
    if late is not None:
        reduce_late.arrive()
        ol[...] = jnp.sum(rl[...].astype(F32), axis=0).astype(BF16)
        send_late = Exchange("ctx", n, rows(ol), rows(bl), bl.at[:most], *pair())
        send_late.start()
        bl[own, :] = ol[own, :]

    d0 = jnp.zeros((tokens, cw), F32)
    d1 = jnp.zeros((tokens, cw), F32)

    def combine(h, d0, d1):
        send_y[h].arrive()
        y0, y1 = dot(p0s[...], by[h]), dot(p1s[...], by[h])
        for k in range(m):
            a, b = y0[:, spans(h, k)], y1[:, spans(h, k)]
            zy[h, k] = (a * gc[0, :, :cw] + b * gc[1, :, :cw]).astype(BF16)
            cot = cots[h, k].astype(F32)
            d0, d1 = d0 + a * cot, d1 + b * cot
        sum_y.append(
            Exchange("exp", m, lambda p, h=h: zy.at[h, p], lambda s, h=h: ry.at[h, s], ry.at[h, :m - 1], *pair())
        )
        sum_y[h].start()
        ry[h, mine] = zy[h, mine]
        return d0, d1

    for h in range(nc):
        d0, d1 = combine(h, d0, d1)
    for h in direct:
        sum_dx[h].arrive()
    sum_norm.arrive()
    if late is not None:
        send_late.arrive()
    q = column(jnp.sum(norm[...], axis=0)[:1])
    scale = sc[...]
    pull = q * scale * scale * scale / width
    for h in range(nc):
        lanes = slice(h * cw, (h + 1) * cw)
        dn = dot(pb[...], bl[...]) if h == late else jnp.sum(rdx[h].astype(F32), axis=0)
        mixed = mx[h, mine].astype(F32)
        dm = cots[h, mine].astype(F32) + gain_row[:, lanes] * dn * scale[:, :cw] - mixed * pull[:, :cw]
        dmp[EDGE : EDGE + tokens, lanes] = dm
        de[0, :, lanes] = dm[:EDGE].astype(BF16)
        de[1, :, lanes] = dm[tokens - EDGE :].astype(BF16)
        tp[me, taps : taps + 1, lanes] = jnp.sum(
            dn * mixed * scale[:, :cw], axis=0, keepdims=True
        ).astype(BF16)
    halo_d = Halo(n, de, dl, dr, hs2)
    halo_d.start()
    for h in range(nc):
        lanes = slice(h * cw, (h + 1) * cw)
        dm = dmp[EDGE : EDGE + tokens, lanes]
        for j in range(taps):
            o = base + j
            b = o % 8
            term = jnp.sum(dm * xs[b, o - b : o - b + tokens, lanes], axis=0, keepdims=True)
            tp[me, j : j + 1, lanes] = term.astype(BF16)
    sum_taps = Exchange("ctx", n, lambda p: tp.at[me], lambda s: tp.at[s], tp.at[:n - 1], *pair())
    sum_taps.start()
    dots[mine, 0:1, :] = turn_row(jnp.sum(d0, axis=1, keepdims=True))
    dots[mine, 1:2, :] = turn_row(jnp.sum(d1, axis=1, keepdims=True))
    sum_dots = Exchange("exp", m, lambda p: dots.at[mine], lambda s: dots.at[s], dots.at[:m - 1], *pair())
    sum_dots.start()

    halo_d.arrive()
    dmp[:EDGE, :] = dl[...].astype(F32)
    dmp[EDGE + tokens :, :] = dr[...].astype(F32)
    low = EDGE + taps // 2 - (taps - 1)
    for h in range(nc):
        lanes = slice(h * cw, (h + 1) * cw)
        block = dmp[:, lanes]
        acc = dmp[EDGE : EDGE + tokens, lanes]
        for b, moved, offs in windows(block, low, taps):
            for o in offs:
                j = EDGE + taps // 2 - o
                acc = acc + tap_s[j : j + 1, lanes] * moved[o - b : o - b + tokens]
        gin_ref[lanes, :] = jnp.transpose(acc).astype(BF16)
    for h in range(nc):
        sum_y[h].arrive()
        out = mx[h, mine].astype(F32) + jnp.sum(ry[h].astype(F32), axis=0)
        lo_ref[h * cw : (h + 1) * cw, :] = jnp.transpose(out).astype(BF16)
    sum_dots.arrive()
    gateo_ref[...] = jnp.sum(dots[...], axis=0)[:2]
    sum_taps.arrive()
    grads = jnp.sum(tp[...].astype(F32), axis=0)
    tapo_ref[...] = grads[:taps]
    gaino_ref[...] = grads[taps : taps + 1]
    singles = [halo, halo_d, share, sum_norm, sum_dots, sum_taps]
    if late is not None:
        singles += [reduce_late, send_late, launch_x, gather_late]
    for group in (singles, gather_cot, gather_mixed, send_x, send_dy, send_dx, send_y, sum_dx, sum_y):
        for done in group:
            done.sent()


def finish(*refs):
    count = (len(refs) - 1) // 2
    sem = refs[-1]
    copies = [
        pltpu.make_async_copy(refs[i], refs[count + i], sem.at[i]) for i in range(count)
    ]
    for copy in copies:
        copy.start()
    for copy in copies:
        copy.wait()


def local(inputs, conv_taps, norm_gain, routes, gate_probs, w_gate, w_up, w_down, grad_out):
    chans, tokens = inputs.shape
    taps = conv_taps.shape[1]
    width, inner = w_gate.shape[1:]
    n, m = lax.axis_size("ctx"), lax.axis_size("exp")
    cap = max(tokens // 8, (2 * tokens + n - 1) // n)
    slots = n * cap
    pad = -(-(taps + 1) // 16) * 16
    nc = 2 if chans % 256 == 0 else 1
    cw = chans // nc
    vmem = pl.BlockSpec(memory_space=pltpu.VMEM)
    hbm = pl.BlockSpec(memory_space=pltpu.HBM)
    shape = jax.ShapeDtypeStruct
    dma = pltpu.SemaphoreType.DMA
    V = pltpu.VMEM
    outs = (
        shape((chans, tokens), BF16),
        shape((chans, tokens), BF16),
        shape((taps, chans), F32),
        shape((1, chans), F32),
        shape((2, tokens), F32),
        shape((width, inner), BF16),
        shape((width, inner), BF16),
        shape((inner, width), BF16),
    )
    straight = nc - 1 if nc > 1 else 1
    extra = nc > 1
    big = V((nc, slots, m * cw), BF16)
    part = V((nc, slots, m * cw), BF16)
    plus = V((straight, slots, m * cw + 128 * extra), BF16)
    operands = [
        pltpu.with_memory_space_constraint(a, pltpu.HBM)
        for a in (
            inputs, conv_taps.T, norm_gain, routes.T, gate_probs.T, grad_out, w_gate, w_up, w_down
        )
    ]
    results = pl.pallas_call(
        functools.partial(layer, n, m, taps, cap, nc),
        out_shape=outs,
        in_specs=[hbm] * 9,
        out_specs=(vmem,) * 8,
        scratch_shapes=[
            V((chans, tokens), BF16), V((taps, chans), F32), V((chans,), BF16),
            V((2, tokens), jnp.int32), V((2, tokens), F32), V((chans, tokens), BF16),
            V((width, inner), BF16), V((width, inner), BF16), V((inner, width), BF16),
            V((tokens + 2 * EDGE, chans), F32), V((8, tokens + 24, chans), F32),
            V((2, EDGE, chans), BF16), V((EDGE, chans), BF16), V((EDGE, chans), BF16),
            V((nc, m, tokens, cw), BF16), V((nc, m, tokens, cw), BF16),
            V((m, 8, max(tokens, cw)), F32),
            V((slots, tokens), BF16), V((tokens, slots), BF16), V((tokens, slots), BF16),
            V((tokens, slots), BF16),
            V((slots, 128), F32), V((2, tokens, 128), F32), V((tokens, 128), F32),
            big, part, big, V((slots, width), BF16), V((slots, cw), BF16), part, V((m, slots, cw), BF16),
            V((slots, inner), F32), V((slots, inner), F32), V((slots, inner), F32),
            V((slots, inner), BF16), V((slots, inner), BF16), V((slots, inner), BF16),
            plus, big, plus, big,
            V((m, slots, cw), BF16), V((m, slots, cw), BF16), V((slots, cw), BF16), V((slots, cw), BF16),
            V((nc, m, tokens, cw), BF16), V((nc, m, tokens, cw), BF16),
            V((nc, m, tokens, cw), BF16), V((nc, m, tokens, cw), BF16),
            V((m, 8, tokens), F32), V((m, 8, tokens), F32),
            V((tokens + 2 * EDGE, chans), F32),
            V((2, EDGE, chans), BF16), V((EDGE, chans), BF16), V((EDGE, chans), BF16),
            V((n, pad, chans), BF16),
            dma((9,)), dma((4,)), dma((4,)),
            dma((64,)),
        ],
        compiler_params=pltpu.CompilerParams(
            collective_id=0, has_side_effects=True, vmem_limit_bytes=36 << 20
        ),
        cost_estimate=pl.CostEstimate(
            flops=18 * slots * width * inner, bytes_accessed=12 * width * inner, transcendentals=slots * inner
        ),
        name="layer",
    )(*operands)
    results = pl.pallas_call(
        finish,
        out_shape=outs,
        in_specs=[vmem] * 8,
        out_specs=(hbm,) * 8,
        scratch_shapes=[dma((8,))],
        compiler_params=pltpu.CompilerParams(vmem_limit_bytes=16 << 20),
        name="finish",
    )(*results)
    layer_out, grad_in, grad_taps, grad_gain, grad_gates, grad_gate, grad_up, grad_down = results
    return (
        layer_out,
        grad_in,
        grad_taps.T,
        grad_gain[0],
        grad_gates.T,
        grad_gate[None],
        grad_up[None],
        grad_down[None],
    )


def solution(mesh):
    return jax.shard_map(
        local,
        mesh=mesh,
        in_specs=(
            P("exp", "ctx"),
            P("exp", None),
            P("exp"),
            P("ctx", None),
            P("ctx", None),
            P("ctx", None, "exp"),
            P("ctx", None, "exp"),
            P("ctx", "exp", None),
            P("exp", "ctx"),
        ),
        out_specs=(
            P("exp", "ctx"),
            P("exp", "ctx"),
            P("exp", None),
            P("exp"),
            P("ctx", None),
            P("ctx", None, "exp"),
            P("ctx", None, "exp"),
            P("ctx", "exp", None),
        ),
        check_vma=False,
    )
```

```python
import functools
import jax
import jax.numpy as jnp
from jax import lax
from jax.experimental import pallas as pl
from jax.experimental.pallas import tpu as pltpu
from jax.sharding import PartitionSpec as P

EPS = 1e-05
EDGE = 16
MESH = pl.DeviceIdType.MESH
F32, BF16 = jnp.float32, jnp.bfloat16
LAST = (((1,), (1,)), ((), ()))
FIRST = (((0,), (0,)), ((), ()))


def dot(a, b, dims=(((1,), (0,)), ((), ()))):
    return lax.dot_general(a, b, dims, preferred_element_type=F32)


def announce(n, m):
    c, e = lax.axis_index("ctx"), lax.axis_index("exp")
    barrier = pltpu.get_barrier_semaphore()

    def ctx_peer(k, _):
        pl.semaphore_signal(barrier, inc=1, device_id=(lax.rem(c + k, n), e), device_id_type=MESH)
        return 0

    def exp_peer(k, _):
        pl.semaphore_signal(barrier, inc=1, device_id=(c, lax.rem(e + k, m)), device_id_type=MESH)
        return 0

    lax.fori_loop(1, n, ctx_peer, 0)
    lax.fori_loop(1, m, exp_peer, 0)
    return barrier


class Exchange:
    def __init__(self, axis, size, src, dst, bulk, send, recv):
        self.axis, self.size, self.src, self.dst = axis, size, src, dst
        self.bulk, self.send, self.recv = bulk, send, recv
        self.me = lax.axis_index(axis)

    def where(self, peer):
        if self.axis == "ctx":
            return peer, lax.axis_index("exp")
        return lax.axis_index("ctx"), peer

    def copy(self, peer, src, dst):
        return pltpu.make_async_remote_copy(
            src_ref=src,
            dst_ref=dst,
            send_sem=self.send,
            recv_sem=self.recv,
            device_id=self.where(peer),
            device_id_type=MESH,
        )

    def start(self):
        def body(k, _):
            peer = lax.rem(self.me + k, self.size)
            self.copy(peer, self.src(peer), self.dst(self.me)).start()
            return 0

        lax.fori_loop(1, self.size, body, 0)

    def all_of_them(self):
        return self.copy(lax.rem(self.me + 1, self.size), self.bulk, self.bulk)

    def arrive(self):
        self.all_of_them().wait_recv()

    def sent(self):
        self.all_of_them().wait_send()


class Halo:
    def __init__(self, n, edges, left, right, sems):
        c, e = lax.axis_index("ctx"), lax.axis_index("exp")
        up, down = lax.rem(c + 1, n), lax.rem(c + n - 1, n)
        make = pltpu.make_async_remote_copy
        self.copies = [
            make(edges.at[1], left, sems.at[0], sems.at[1], device_id=(up, e), device_id_type=MESH),
            make(edges.at[0], right, sems.at[2], sems.at[3], device_id=(down, e), device_id_type=MESH),
        ]

    def start(self):
        for copy in self.copies:
            copy.start()

    def arrive(self):
        for copy in self.copies:
            copy.wait_recv()

    def sent(self):
        for copy in self.copies:
            copy.wait_send()


def column(row):
    return jnp.transpose(jnp.broadcast_to(row, (128, row.shape[1])))


def turn_row(col):
    return jnp.transpose(jnp.broadcast_to(col, (col.shape[0], 128)))[:1]


def windows(block, base, taps):
    rows = block.shape[0]
    for b in range(8):
        offs = [o for o in range(base, base + taps) if o % 8 == b]
        if offs:
            yield b, (block if b == 0 else pltpu.roll(block, rows - b, axis=0)), offs


def layer(n, m, taps, cap, nc,
          x_any, tap_any, gain_any, route_any, prob_any, cot_any, wg_any, wu_any, wd_any,
          lo_ref, gin_ref, tapo_ref, gaino_ref, gateo_ref, gwg_ref, gwu_ref, gwd_ref,
          x_s, tap_s, gain_s, route_s, prob_s, cot_s, wg, wu, wd,
          xp, xs, xe, hl, hr, cots, mx, side, pt, pb, p0s, p1s, gs, gc, sc,
          sdy, sx, rdy, rx, sxl, xa, xg, gained, unit, dh, ga, ua, hid, dg, du, sdx, sy, bdx, by, sl, rl, ol, bl,
          zdx, zy, rdx, ry, dots, norm, dmp, de, dl, dr, tp,
          lsem, hs, hs2, sem):
    me, mine = lax.axis_index("ctx"), lax.axis_index("exp")
    chans, tokens = x_s.shape
    slots = pt.shape[0]
    width, inner = wg.shape
    cw = chans // nc
    it = iter(range(sem.shape[0]))
    own = pl.ds(pl.multiple_of(me * cap, cap), cap)
    most = (n - 1) * cap
    late = nc - 1 if nc > 1 else None
    direct = [h for h in range(nc) if h != late]
    span_all = m * cw

    def pair():
        return sem.at[next(it)], sem.at[next(it)]

    def spans(h, k):
        return slice(k * cw, (k + 1) * cw)

    def natural(ref, lo, hi):
        if nc == 1:
            return ref[0, :, lo:hi]
        return jnp.concatenate(
            [ref[h, :, spans(h, k)] for k in range(lo // chans, hi // chans) for h in range(nc)], axis=1
        )

    def rows(ref, *h):
        return lambda p: ref.at[(*h, pl.ds(pl.multiple_of(p * cap, cap), cap))]

    def gain_of(k, h):
        return side[k, 1 + h : 2 + h, :cw]

    def spread(matrix, pieces):
        if cw % 128 == 0:
            full = dot(matrix, jnp.concatenate(pieces, axis=1))
            return [full[:, k * cw : (k + 1) * cw] for k in range(len(pieces))]
        return [dot(matrix, piece) for piece in pieces]

    barrier = announce(n, m)
    loads = [
        pltpu.make_async_copy(src, dst, lsem.at[i])
        for i, (src, dst) in enumerate(
            [(x_any, x_s), (cot_any, cot_s), (route_any, route_s), (prob_any, prob_s),
             (tap_any, tap_s), (gain_any, gain_s)]
        )
    ]
    weights = [
        pltpu.make_async_copy(src.at[0], dst, lsem.at[6 + i])
        for i, (src, dst) in enumerate([(wd_any, wd), (wg_any, wg), (wu_any, wu)])
    ]
    for load in loads:
        load.start()
    for load in weights:
        load.start()
    loads[0].wait()
    loads[1].wait()
    x_t = jnp.transpose(x_s[...].astype(F32))
    xp[EDGE : EDGE + tokens, :] = x_t
    xe[0] = x_t[:EDGE].astype(BF16)
    xe[1] = x_t[tokens - EDGE :].astype(BF16)
    cot_t = jnp.transpose(cot_s[...].astype(F32)).astype(BF16)
    for h in range(nc):
        cots[h, mine] = cot_t[:, h * cw : (h + 1) * cw]
    pl.semaphore_wait(barrier, n + m - 2)

    halo = Halo(n, xe, hl, hr, hs)
    halo.start()
    gather_cot = []
    for h in range(nc):
        gather_cot.append(
            Exchange("exp", m, lambda p, h=h: cots.at[h, mine], lambda s, h=h: cots.at[h, s], cots.at[h, :m - 1], *pair())
        )
    for h in range(nc):
        gather_cot[h].start()

    for load in loads[2:]:
        load.wait()
    ids = lax.broadcasted_iota(jnp.int32, (n, tokens), 0)
    named = [route_s[k : k + 1, :] for k in range(2)]
    probs = [prob_s[k : k + 1, :] for k in range(2)]
    hot = [(ids == r).astype(F32) for r in named]
    earlier = lax.broadcasted_iota(jnp.int32, (tokens, tokens), 0) < lax.broadcasted_iota(
        jnp.int32, (tokens, tokens), 1
    )
    count = dot((hot[0] + hot[1]).astype(BF16), earlier.astype(F32).astype(BF16))
    place = lax.broadcasted_iota(jnp.int32, (slots, tokens), 0)
    picks = []
    for r, one in zip(named, hot):
        slot = jnp.sum(count * one, axis=0, keepdims=True).astype(jnp.int32)
        picks.append((place == r * cap + slot).astype(F32))
    pt[...] = (picks[0] + picks[1]).astype(BF16)
    gate_slot = jnp.sum(picks[0] * probs[0] + picks[1] * probs[1], axis=1, keepdims=True)
    gs[...] = jnp.broadcast_to(gate_slot, gs.shape)
    turned = [jnp.transpose(p) for p in picks]
    p0s[...] = turned[0].astype(BF16)
    p1s[...] = turned[1].astype(BF16)
    pb[...] = (turned[0] + turned[1]).astype(BF16)
    gc[0] = column(probs[0])
    gc[1] = column(probs[1])
    gain_row = gain_s[...].astype(F32).reshape(1, chans)
    side[mine] = jnp.zeros(side.shape[1:], F32)
    dots[mine] = jnp.zeros(dots.shape[1:], F32)

    halo.arrive()
    xp[:EDGE, :] = hl[...].astype(F32)
    xp[EDGE + tokens :, :] = hr[...].astype(F32)
    base = EDGE - taps // 2
    span = tokens + 24
    gather_mixed = []

    def begin_mixed():
        for h in direct:
            gather_mixed.append(
                Exchange("exp", m, lambda p, h=h: mx.at[h, mine], lambda s, h=h: mx.at[h, s], mx.at[h, :m - 1], *pair())
            )
            gather_mixed[h].start()


    squares = jnp.zeros((tokens, 1), F32)
    for h in range(nc):
        lanes = slice(h * cw, (h + 1) * cw)
        block = xp[:, lanes]
        acc = xp[EDGE : EDGE + tokens, lanes]
        for b, moved, offs in windows(block, base, taps):
            xs[b, :, lanes] = moved[:span]
            for o in offs:
                acc = acc + tap_s[o - base : o - base + 1, lanes] * moved[o - b : o - b + tokens]
        mixed = acc.astype(BF16)
        mx[h, mine] = mixed
        mixed = mixed.astype(F32)
        squares = squares + jnp.sum(mixed * mixed, axis=1, keepdims=True)
        side[mine, 1 + h : 2 + h, :cw] = gain_row[:, lanes]
    side[mine, 0:1, :tokens] = turn_row(squares)
    share = Exchange("exp", m, lambda p: side.at[mine], lambda s: side.at[s], side.at[:m - 1], *pair())
    share.start()
    if late is not None:
        sxl[...] = dot(pt[...], mx[late, mine]).astype(BF16)
        launch_x = Exchange("ctx", n, rows(sxl), rows(xg, mine), xg.at[mine, :most], *pair())
        launch_x.start()
        xg[mine, own, :] = sxl[own, :]

    begin_mixed()
    send_dy = []

    def dispatch_cot(h):
        gather_cot[h].arrive()
        for k, part in enumerate(spread(pt[...], [cots[h, k] for k in range(m)])):
            sdy[h, :, spans(h, k)] = (part * gs[:, :cw]).astype(BF16)
        send_dy.append(Exchange("ctx", n, rows(sdy, h), rows(rdy, h), rdy.at[h, :most], *pair()))
        send_dy[h].start()
        rdy[h, own, :] = sdy[h, own, :]

    if late is not None:
        gather_late = Exchange("exp", m, lambda p: xg.at[mine], lambda s: xg.at[s], xg.at[:m - 1], *pair())
    dispatch_cot(0)
    if late is not None:
        launch_x.arrive()
        gather_late.start()
    for h in range(1, nc):
        dispatch_cot(h)
    share.arrive()
    total = jnp.sum(side[...], axis=0)[:1, :tokens]
    sc[...] = column(lax.rsqrt(total / width + EPS))
    send_x = []
    for h in direct:
        gather_mixed[h].arrive()
        for k, part in enumerate(spread(pt[...], [mx[h, k] for k in range(m)])):
            sx[h, :, spans(h, k)] = part.astype(BF16)
        send_x.append(Exchange("ctx", n, rows(sx, h), rows(xa, h), xa.at[h, :most], *pair()))
        send_x[h].start()
        xa[h, own, :] = sx[h, own, :]

    tile = min(256, inner)
    tiles = [slice(f, f + tile) for f in range(0, inner, tile)]
    step = 32

    def raw(k, h, at):
        return (xg[k, at, :] if h == late else xa[h, at, spans(h, k)]).astype(F32)

    def weigh(h):
        for r in range(0, slots, step):
            at = slice(r, r + step)
            acc = jnp.zeros((step, cw), F32)
            for k in range(m):
                part = raw(k, h, at)
                acc = acc + part * part
                gained[h, at, spans(h, k)] = (part * gain_of(k, h)).astype(BF16)
            total = jnp.broadcast_to(jnp.sum(acc, axis=1, keepdims=True), (step, 128))
            unit[at] = total if h == first else unit[at] + total

    def chan_rows(ref, h, cols):
        if nc == 1:
            return ref[:, cols]
        return jnp.concatenate(
            [ref[k * chans + h * cw : k * chans + (h + 1) * cw, cols] for k in range(m)], axis=0
        )

    def project(h, f):
        for ref, w in ((ga, wg), (ua, wu)):
            part = dot(gained[h], chan_rows(w, h, f))
            ref[:, f] = part if h == first else ref[:, f] + part

    weights[0].wait()
    weights[1].wait()
    weights[2].wait()
    first = direct[0] if late is None else late
    if late is not None:
        gather_late.arrive()
        weigh(late)
        for f in tiles:
            project(late, f)
    for h in range(nc):
        send_dy[h].arrive()
    d_y = natural(rdy, 0, width)
    for f in tiles:
        dh[:, f] = dot(d_y, wd[f, :], LAST)
    for h in direct:
        send_x[h].arrive()
        weigh(h)
    unit[...] = lax.rsqrt(unit[...] / width + EPS)
    for f in tiles:
        for h in direct:
            project(h, f)
        for r in range(0, slots, step):
            at = slice(r, r + step)
            each = jnp.concatenate([unit[at]] * (tile // 128), axis=1)
            g, u, d = ga[at, f] * each, ua[at, f] * each, dh[at, f]
            sigma = jax.nn.sigmoid(g)
            swish = g * sigma
            hid[at, f] = (swish * u).astype(BF16)
            dg[at, f] = (d * u * sigma * (1.0 + g * (1.0 - sigma))).astype(BF16)
            du[at, f] = (d * swish).astype(BF16)
    group = max(1, min(m, 256 // cw))
    def row_grads(h):
        for k in range(0, m, group):
            if nc == 1:
                at = slice(k * cw, (k + group) * cw)
                w1, w2 = wg[at, :], wu[at, :]
            else:
                w1, w2 = [
                    jnp.concatenate(
                        [w[j * chans + h * cw : j * chans + (h + 1) * cw, :] for j in range(k, k + group)], axis=0
                    )
                    for w in (wg, wu)
                ]
            yield k, dot(dg[...], w1, LAST) + dot(du[...], w2, LAST)

    send_dx, send_y = [], []
    if late is not None:
        inner_q = jnp.zeros((slots, cw), F32)
        for k, part in row_grads(late):
            for j in range(k, k + group):
                piece = part[:, (j - k) * cw : (j - k + 1) * cw]
                sl[j] = piece.astype(BF16)
                inner_q = inner_q + piece * raw(j, late, slice(None)) * gain_of(j, late)
        reduce_late = Exchange("exp", m, lambda p: sl.at[p], lambda s: rl.at[s], rl.at[:m - 1], *pair())
        reduce_late.start()
        rl[mine] = sl[mine]
        inner_q = jnp.sum(inner_q, axis=1, keepdims=True)
        high = inner_q.astype(BF16).astype(F32)
        lane = lax.broadcasted_iota(jnp.int32, (slots, 128), 1)
        sdx[0, :, span_all:] = jnp.where(
            lane == 0, high, jnp.where(lane == 1, inner_q - high, 0.0)
        ).astype(BF16)
    def act_dx():
        for h in direct:
            for k, part in row_grads(h):
                sdx[h, :, k * cw : (k + group) * cw] = part.astype(BF16)
            send_dx.append(Exchange("ctx", n, rows(sdx, h), rows(bdx, h), bdx.at[h, :most], *pair()))
            send_dx[h].start()
            bdx[h, own, :] = sdx[h, own, :]
    def act_y(h):
        for k in range(0, m, group):
            if nc == 1:
                w = wd[:, k * cw : (k + group) * cw]
            else:
                w = jnp.concatenate(
                    [wd[:, j * chans + h * cw : j * chans + (h + 1) * cw] for j in range(k, k + group)], axis=1
                )
            sy[h, :, k * cw : (k + group) * cw] = dot(hid[...], w).astype(BF16)
        send_y.append(Exchange("ctx", n, rows(sy, h), rows(by, h), by.at[h, :most], *pair()))
        send_y[h].start()
        by[h, own, :] = sy[h, own, :]

    def act_grads(part):
        if part == 0:
            for f in tiles:
                gwd_ref[f, :] = dot(hid[:, f], natural(rdy, 0, width), FIRST).astype(BF16)
        if part == 1:
            for r in range(0, slots, step):
                at = slice(r, r + step)
                for k in range(m):
                    for h in range(nc):
                        lo = k * chans + h * cw
                        normed = raw(k, h, at) * gain_of(k, h) * unit[at, :cw]
                        rx[at, lo : lo + cw] = normed.astype(BF16)
            for lo in range(0, width, 256):
                part = rx[:, lo : lo + 256]
                gwg_ref[lo : lo + 256, :] = dot(part, dg[...], FIRST).astype(BF16)
                gwu_ref[lo : lo + 256, :] = dot(part, du[...], FIRST).astype(BF16)

    act_dx()
    act_y(0)
    act_grads(0)
    act_grads(1)
    for h in range(1, nc):
        act_y(h)

    sum_dx, sum_y = [], []
    weighted = jnp.zeros((tokens, cw), F32)
    sum_norm = Exchange("exp", m, lambda p: norm.at[mine], lambda s: norm.at[s], norm.at[:m - 1], *pair())
    for h in direct:
        send_dx[h].arrive()
        full = dot(pb[...], bdx[h])
        if h == 0 and late is not None:
            late_q = full[:, span_all : span_all + 1] + full[:, span_all + 1 : span_all + 2]
        for k in range(m):
            part = full[:, spans(h, k)]
            zdx[h, k] = part.astype(BF16)
            weighted = weighted + part * mx[h, k].astype(F32) * gain_of(k, h)
        if h == direct[-1]:
            total_q = jnp.sum(weighted, axis=1, keepdims=True)
            if late is not None:
                total_q = total_q + late_q
            norm[mine] = jnp.broadcast_to(turn_row(total_q), norm.shape[1:])
            sum_norm.start()
        sum_dx.append(
            Exchange("exp", m, lambda p, h=h: zdx.at[h, p], lambda s, h=h: rdx.at[h, s], rdx.at[h, :m - 1], *pair())
        )
        sum_dx[h].start()
        rdx[h, mine] = zdx[h, mine]
    def combine(h, d0, d1):
        send_y[h].arrive()
        y0, y1 = dot(p0s[...], by[h]), dot(p1s[...], by[h])
        for k in range(m):
            a, b = y0[:, spans(h, k)], y1[:, spans(h, k)]
            zy[h, k] = (a * gc[0, :, :cw] + b * gc[1, :, :cw]).astype(BF16)
            cot = cots[h, k].astype(F32)
            d0, d1 = d0 + a * cot, d1 + b * cot
        sum_y.append(
            Exchange("exp", m, lambda p, h=h: zy.at[h, p], lambda s, h=h: ry.at[h, s], ry.at[h, :m - 1], *pair())
        )
        sum_y[h].start()
        ry[h, mine] = zy[h, mine]
        return d0, d1

    d0 = jnp.zeros((tokens, cw), F32)
    d1 = jnp.zeros((tokens, cw), F32)
    if late is not None:
        reduce_late.arrive()
        ol[...] = jnp.sum(rl[...].astype(F32), axis=0).astype(BF16)
        send_late = Exchange("ctx", n, rows(ol), rows(bl), bl.at[:most], *pair())
        send_late.start()
        bl[own, :] = ol[own, :]

    for h in range(nc):
        d0, d1 = combine(h, d0, d1)
    for h in direct:
        sum_dx[h].arrive()
    sum_norm.arrive()
    if late is not None:
        send_late.arrive()
    q = column(jnp.sum(norm[...], axis=0)[:1])
    scale = sc[...]
    pull = q * scale * scale * scale / width
    for h in range(nc):
        lanes = slice(h * cw, (h + 1) * cw)
        dn = dot(pb[...], bl[...]) if h == late else jnp.sum(rdx[h].astype(F32), axis=0)
        mixed = mx[h, mine].astype(F32)
        dm = cots[h, mine].astype(F32) + gain_row[:, lanes] * dn * scale[:, :cw] - mixed * pull[:, :cw]
        dmp[EDGE : EDGE + tokens, lanes] = dm
        de[0, :, lanes] = dm[:EDGE].astype(BF16)
        de[1, :, lanes] = dm[tokens - EDGE :].astype(BF16)
        tp[me, taps : taps + 1, lanes] = jnp.sum(
            dn * mixed * scale[:, :cw], axis=0, keepdims=True
        ).astype(BF16)
    halo_d = Halo(n, de, dl, dr, hs2)
    halo_d.start()
    for h in range(nc):
        lanes = slice(h * cw, (h + 1) * cw)
        dm = dmp[EDGE : EDGE + tokens, lanes]
        for j in range(taps):
            o = base + j
            b = o % 8
            term = jnp.sum(dm * xs[b, o - b : o - b + tokens, lanes], axis=0, keepdims=True)
            tp[me, j : j + 1, lanes] = term.astype(BF16)
    sum_taps = Exchange("ctx", n, lambda p: tp.at[me], lambda s: tp.at[s], tp.at[:n - 1], *pair())
    sum_taps.start()
    dots[mine, 0:1, :] = turn_row(jnp.sum(d0, axis=1, keepdims=True))
    dots[mine, 1:2, :] = turn_row(jnp.sum(d1, axis=1, keepdims=True))
    sum_dots = Exchange("exp", m, lambda p: dots.at[mine], lambda s: dots.at[s], dots.at[:m - 1], *pair())
    sum_dots.start()

    halo_d.arrive()
    dmp[:EDGE, :] = dl[...].astype(F32)
    dmp[EDGE + tokens :, :] = dr[...].astype(F32)
    low = EDGE + taps // 2 - (taps - 1)
    for h in range(nc):
        lanes = slice(h * cw, (h + 1) * cw)
        block = dmp[:, lanes]
        acc = dmp[EDGE : EDGE + tokens, lanes]
        for b, moved, offs in windows(block, low, taps):
            for o in offs:
                j = EDGE + taps // 2 - o
                acc = acc + tap_s[j : j + 1, lanes] * moved[o - b : o - b + tokens]
        gin_ref[lanes, :] = jnp.transpose(acc).astype(BF16)
    sum_taps.arrive()
    grads = jnp.sum(tp[...].astype(F32), axis=0)
    tapo_ref[...] = grads[:taps]
    gaino_ref[...] = grads[taps : taps + 1]
    for h in range(nc):
        sum_y[h].arrive()
        out = mx[h, mine].astype(F32) + jnp.sum(ry[h].astype(F32), axis=0)
        lo_ref[h * cw : (h + 1) * cw, :] = jnp.transpose(out).astype(BF16)
    sum_dots.arrive()
    gateo_ref[...] = jnp.sum(dots[...], axis=0)[:2]
    singles = [halo, halo_d, share, sum_norm, sum_dots, sum_taps]
    if late is not None:
        singles += [reduce_late, send_late, launch_x, gather_late]
    for group in (singles, gather_cot, gather_mixed, send_x, send_dy, send_dx, send_y, sum_dx, sum_y):
        for done in group:
            done.sent()


def finish(*refs):
    count = (len(refs) - 1) // 2
    sem = refs[-1]
    copies = [
        pltpu.make_async_copy(refs[i], refs[count + i], sem.at[i]) for i in range(count)
    ]
    for copy in copies:
        copy.start()
    for copy in copies:
        copy.wait()


def local(inputs, conv_taps, norm_gain, routes, gate_probs, w_gate, w_up, w_down, grad_out):
    chans, tokens = inputs.shape
    taps = conv_taps.shape[1]
    width, inner = w_gate.shape[1:]
    n, m = lax.axis_size("ctx"), lax.axis_size("exp")
    cap = max(tokens // 8, (2 * tokens + n - 1) // n)
    slots = n * cap
    pad = -(-(taps + 1) // 16) * 16
    nc = 2 if chans % 256 == 0 else 1
    cw = chans // nc
    vmem = pl.BlockSpec(memory_space=pltpu.VMEM)
    hbm = pl.BlockSpec(memory_space=pltpu.HBM)
    shape = jax.ShapeDtypeStruct
    dma = pltpu.SemaphoreType.DMA
    V = pltpu.VMEM
    outs = (
        shape((chans, tokens), BF16),
        shape((chans, tokens), BF16),
        shape((taps, chans), F32),
        shape((1, chans), F32),
        shape((2, tokens), F32),
        shape((width, inner), BF16),
        shape((width, inner), BF16),
        shape((inner, width), BF16),
    )
    straight = nc - 1 if nc > 1 else 1
    extra = nc > 1
    big = V((nc, slots, m * cw), BF16)
    part = V((nc, slots, m * cw), BF16)
    plus = V((straight, slots, m * cw + 128 * extra), BF16)
    operands = [
        pltpu.with_memory_space_constraint(a, pltpu.HBM)
        for a in (
            inputs, conv_taps.T, norm_gain, routes.T, gate_probs.T, grad_out, w_gate, w_up, w_down
        )
    ]
    results = pl.pallas_call(
        functools.partial(layer, n, m, taps, cap, nc),
        out_shape=outs,
        in_specs=[hbm] * 9,
        out_specs=(vmem,) * 8,
        scratch_shapes=[
            V((chans, tokens), BF16), V((taps, chans), F32), V((chans,), BF16),
            V((2, tokens), jnp.int32), V((2, tokens), F32), V((chans, tokens), BF16),
            V((width, inner), BF16), V((width, inner), BF16), V((inner, width), BF16),
            V((tokens + 2 * EDGE, chans), F32), V((8, tokens + 24, chans), F32),
            V((2, EDGE, chans), BF16), V((EDGE, chans), BF16), V((EDGE, chans), BF16),
            V((nc, m, tokens, cw), BF16), V((nc, m, tokens, cw), BF16),
            V((m, 8, max(tokens, cw)), F32),
            V((slots, tokens), BF16), V((tokens, slots), BF16), V((tokens, slots), BF16),
            V((tokens, slots), BF16),
            V((slots, 128), F32), V((2, tokens, 128), F32), V((tokens, 128), F32),
            big, part, big, V((slots, width), BF16), V((slots, cw), BF16), part, V((m, slots, cw), BF16), big, V((slots, 128), F32),
            V((slots, inner), F32), V((slots, inner), F32), V((slots, inner), F32),
            V((slots, inner), BF16), V((slots, inner), BF16), V((slots, inner), BF16),
            plus, big, plus, big,
            V((m, slots, cw), BF16), V((m, slots, cw), BF16), V((slots, cw), BF16), V((slots, cw), BF16),
            V((nc, m, tokens, cw), BF16), V((nc, m, tokens, cw), BF16),
            V((nc, m, tokens, cw), BF16), V((nc, m, tokens, cw), BF16),
            V((m, 8, tokens), F32), V((m, 8, tokens), F32),
            V((tokens + 2 * EDGE, chans), F32),
            V((2, EDGE, chans), BF16), V((EDGE, chans), BF16), V((EDGE, chans), BF16),
            V((n, pad, chans), BF16),
            dma((9,)), dma((4,)), dma((4,)),
            dma((42,)),
        ],
        compiler_params=pltpu.CompilerParams(
            collective_id=0, has_side_effects=True, vmem_limit_bytes=36 << 20
        ),
        cost_estimate=pl.CostEstimate(
            flops=18 * slots * width * inner, bytes_accessed=12 * width * inner, transcendentals=slots * inner
        ),
        name="layer",
    )(*operands)
    results = pl.pallas_call(
        finish,
        out_shape=outs,
        in_specs=[vmem] * 8,
        out_specs=(hbm,) * 8,
        scratch_shapes=[dma((8,))],
        compiler_params=pltpu.CompilerParams(vmem_limit_bytes=16 << 20),
        name="finish",
    )(*results)
    layer_out, grad_in, grad_taps, grad_gain, grad_gates, grad_gate, grad_up, grad_down = results
    return (
        layer_out,
        grad_in,
        grad_taps.T,
        grad_gain[0],
        grad_gates.T,
        grad_gate[None],
        grad_up[None],
        grad_down[None],
    )


def solution(mesh):
    return jax.shard_map(
        local,
        mesh=mesh,
        in_specs=(
            P("exp", "ctx"),
            P("exp", None),
            P("exp"),
            P("ctx", None),
            P("ctx", None),
            P("ctx", None, "exp"),
            P("ctx", None, "exp"),
            P("ctx", "exp", None),
            P("exp", "ctx"),
        ),
        out_specs=(
            P("exp", "ctx"),
            P("exp", "ctx"),
            P("exp", None),
            P("exp"),
            P("ctx", None),
            P("ctx", None, "exp"),
            P("ctx", None, "exp"),
            P("ctx", "exp", None),
        ),
        check_vma=False,
    )
```

```python
import functools
import jax
import jax.numpy as jnp
from jax import lax
from jax.experimental import pallas as pl
from jax.experimental.pallas import tpu as pltpu
from jax.sharding import PartitionSpec as P

EPS = 1e-05
EDGE = 16
MESH = pl.DeviceIdType.MESH
F32, BF16 = jnp.float32, jnp.bfloat16
LAST = (((1,), (1,)), ((), ()))
FIRST = (((0,), (0,)), ((), ()))


def dot(a, b, dims=(((1,), (0,)), ((), ()))):
    return lax.dot_general(a, b, dims, preferred_element_type=F32)


def announce(n, m):
    c, e = lax.axis_index("ctx"), lax.axis_index("exp")
    barrier = pltpu.get_barrier_semaphore()

    def ctx_peer(k, _):
        pl.semaphore_signal(barrier, inc=1, device_id=(lax.rem(c + k, n), e), device_id_type=MESH)
        return 0

    def exp_peer(k, _):
        pl.semaphore_signal(barrier, inc=1, device_id=(c, lax.rem(e + k, m)), device_id_type=MESH)
        return 0

    lax.fori_loop(1, n, ctx_peer, 0)
    lax.fori_loop(1, m, exp_peer, 0)
    return barrier


class Exchange:
    def __init__(self, axis, size, src, dst, bulk, send, recv):
        self.axis, self.size, self.src, self.dst = axis, size, src, dst
        self.bulk, self.send, self.recv = bulk, send, recv
        self.me = lax.axis_index(axis)

    def where(self, peer):
        if self.axis == "ctx":
            return peer, lax.axis_index("exp")
        return lax.axis_index("ctx"), peer

    def copy(self, peer, src, dst):
        return pltpu.make_async_remote_copy(
            src_ref=src,
            dst_ref=dst,
            send_sem=self.send,
            recv_sem=self.recv,
            device_id=self.where(peer),
            device_id_type=MESH,
        )

    def start(self):
        def body(k, _):
            peer = lax.rem(self.me + k, self.size)
            self.copy(peer, self.src(peer), self.dst(self.me)).start()
            return 0

        lax.fori_loop(1, self.size, body, 0)

    def all_of_them(self):
        return self.copy(lax.rem(self.me + 1, self.size), self.bulk, self.bulk)

    def arrive(self):
        self.all_of_them().wait_recv()

    def sent(self):
        self.all_of_them().wait_send()


class Halo:
    def __init__(self, n, edges, left, right, sems):
        c, e = lax.axis_index("ctx"), lax.axis_index("exp")
        up, down = lax.rem(c + 1, n), lax.rem(c + n - 1, n)
        make = pltpu.make_async_remote_copy
        self.copies = [
            make(edges.at[1], left, sems.at[0], sems.at[1], device_id=(up, e), device_id_type=MESH),
            make(edges.at[0], right, sems.at[2], sems.at[3], device_id=(down, e), device_id_type=MESH),
        ]

    def start(self):
        for copy in self.copies:
            copy.start()

    def arrive(self):
        for copy in self.copies:
            copy.wait_recv()

    def sent(self):
        for copy in self.copies:
            copy.wait_send()


def column(row):
    return jnp.transpose(jnp.broadcast_to(row, (128, row.shape[1])))


def turn_row(col):
    return jnp.transpose(jnp.broadcast_to(col, (col.shape[0], 128)))[:1]


def windows(block, base, taps):
    rows = block.shape[0]
    for b in range(8):
        offs = [o for o in range(base, base + taps) if o % 8 == b]
        if offs:
            yield b, (block if b == 0 else pltpu.roll(block, rows - b, axis=0)), offs


def layer(n, m, taps, cap, nc,
          x_any, tap_any, gain_any, route_any, prob_any, cot_any, wg_any, wu_any, wd_any,
          lo_ref, gin_ref, tapo_ref, gaino_ref, gateo_ref, gwg_ref, gwu_ref, gwd_ref,
          x_s, tap_s, gain_s, route_s, prob_s, cot_s, wg, wu, wd,
          xp, xs, xe, hl, hr, cots, mx, side, pt, pb, p0s, p1s, gs, gc, sc,
          sdy, sx, rdy, rx, sxl, xa, xg, gained, unit, dh, ga, ua, hid, dg, du, sdx, sy, bdx, by, sl, rl, ol, bl,
          zdx, zy, rdx, ry, dots, norm, dmp, de, dl, dr, tp,
          lsem, hs, hs2, sem):
    me, mine = lax.axis_index("ctx"), lax.axis_index("exp")
    chans, tokens = x_s.shape
    slots = pt.shape[0]
    width, inner = wg.shape
    cw = chans // nc
    it = iter(range(sem.shape[0]))
    own = pl.ds(pl.multiple_of(me * cap, cap), cap)
    most = (n - 1) * cap
    late = nc - 1 if nc > 1 else None
    direct = [h for h in range(nc) if h != late]
    span_all = m * cw

    def pair():
        return sem.at[next(it)], sem.at[next(it)]

    def spans(h, k):
        return slice(k * cw, (k + 1) * cw)

    def natural(ref, lo, hi):
        if nc == 1:
            return ref[0, :, lo:hi]
        return jnp.concatenate(
            [ref[h, :, spans(h, k)] for k in range(lo // chans, hi // chans) for h in range(nc)], axis=1
        )

    def rows(ref, *h):
        return lambda p: ref.at[(*h, pl.ds(pl.multiple_of(p * cap, cap), cap))]

    def gain_of(k, h):
        return side[k, 1 + h : 2 + h, :cw]

    def spread(matrix, pieces):
        if cw % 128 == 0:
            full = dot(matrix, jnp.concatenate(pieces, axis=1))
            return [full[:, k * cw : (k + 1) * cw] for k in range(len(pieces))]
        return [dot(matrix, piece) for piece in pieces]

    barrier = announce(n, m)
    loads = [
        pltpu.make_async_copy(src, dst, lsem.at[i])
        for i, (src, dst) in enumerate(
            [(x_any, x_s), (cot_any, cot_s), (route_any, route_s), (prob_any, prob_s),
             (tap_any, tap_s), (gain_any, gain_s)]
        )
    ]
    weights = [
        pltpu.make_async_copy(src.at[0], dst, lsem.at[6 + i])
        for i, (src, dst) in enumerate([(wd_any, wd), (wg_any, wg), (wu_any, wu)])
    ]
    for load in loads:
        load.start()
    for load in weights:
        load.start()
    loads[0].wait()
    loads[1].wait()
    x_t = jnp.transpose(x_s[...].astype(F32))
    xp[EDGE : EDGE + tokens, :] = x_t
    xe[0] = x_t[:EDGE].astype(BF16)
    xe[1] = x_t[tokens - EDGE :].astype(BF16)
    cot_t = jnp.transpose(cot_s[...].astype(F32)).astype(BF16)
    for h in range(nc):
        cots[h, mine] = cot_t[:, h * cw : (h + 1) * cw]
    pl.semaphore_wait(barrier, n + m - 2)

    halo = Halo(n, xe, hl, hr, hs)
    halo.start()
    gather_cot = []
    for h in range(nc):
        gather_cot.append(
            Exchange("exp", m, lambda p, h=h: cots.at[h, mine], lambda s, h=h: cots.at[h, s], cots.at[h, :m - 1], *pair())
        )
    for h in range(nc):
        gather_cot[h].start()

    for load in loads[2:]:
        load.wait()
    ids = lax.broadcasted_iota(jnp.int32, (n, tokens), 0)
    named = [route_s[k : k + 1, :] for k in range(2)]
    probs = [prob_s[k : k + 1, :] for k in range(2)]
    hot = [(ids == r).astype(F32) for r in named]
    earlier = lax.broadcasted_iota(jnp.int32, (tokens, tokens), 0) < lax.broadcasted_iota(
        jnp.int32, (tokens, tokens), 1
    )
    count = dot((hot[0] + hot[1]).astype(BF16), earlier.astype(F32).astype(BF16))
    place = lax.broadcasted_iota(jnp.int32, (slots, tokens), 0)
    picks = []
    for r, one in zip(named, hot):
        slot = jnp.sum(count * one, axis=0, keepdims=True).astype(jnp.int32)
        picks.append((place == r * cap + slot).astype(F32))
    pt[...] = (picks[0] + picks[1]).astype(BF16)
    gate_slot = jnp.sum(picks[0] * probs[0] + picks[1] * probs[1], axis=1, keepdims=True)
    gs[...] = jnp.broadcast_to(gate_slot, gs.shape)
    turned = [jnp.transpose(p) for p in picks]
    p0s[...] = turned[0].astype(BF16)
    p1s[...] = turned[1].astype(BF16)
    pb[...] = (turned[0] + turned[1]).astype(BF16)
    gc[0] = column(probs[0])
    gc[1] = column(probs[1])
    gain_row = gain_s[...].astype(F32).reshape(1, chans)
    side[mine] = jnp.zeros(side.shape[1:], F32)
    dots[mine] = jnp.zeros(dots.shape[1:], F32)

    halo.arrive()
    xp[:EDGE, :] = hl[...].astype(F32)
    xp[EDGE + tokens :, :] = hr[...].astype(F32)
    base = EDGE - taps // 2
    span = tokens + 24
    gather_mixed = []

    def begin_mixed():
        for h in direct:
            gather_mixed.append(
                Exchange("exp", m, lambda p, h=h: mx.at[h, mine], lambda s, h=h: mx.at[h, s], mx.at[h, :m - 1], *pair())
            )
            gather_mixed[h].start()


    squares = jnp.zeros((tokens, 1), F32)
    for h in range(nc):
        lanes = slice(h * cw, (h + 1) * cw)
        block = xp[:, lanes]
        acc = xp[EDGE : EDGE + tokens, lanes]
        for b, moved, offs in windows(block, base, taps):
            xs[b, :, lanes] = moved[:span]
            for o in offs:
                acc = acc + tap_s[o - base : o - base + 1, lanes] * moved[o - b : o - b + tokens]
        mixed = acc.astype(BF16)
        mx[h, mine] = mixed
        mixed = mixed.astype(F32)
        squares = squares + jnp.sum(mixed * mixed, axis=1, keepdims=True)
        side[mine, 1 + h : 2 + h, :cw] = gain_row[:, lanes]
    side[mine, 0:1, :tokens] = turn_row(squares)
    share = Exchange("exp", m, lambda p: side.at[mine], lambda s: side.at[s], side.at[:m - 1], *pair())
    share.start()
    if late is not None:
        sxl[...] = dot(pt[...], mx[late, mine]).astype(BF16)
        launch_x = Exchange("ctx", n, rows(sxl), rows(xg, mine), xg.at[mine, :most], *pair())
        launch_x.start()
        xg[mine, own, :] = sxl[own, :]

    begin_mixed()
    send_dy = []

    def dispatch_cot(h):
        gather_cot[h].arrive()
        for k, part in enumerate(spread(pt[...], [cots[h, k] for k in range(m)])):
            sdy[h, :, spans(h, k)] = (part * gs[:, :cw]).astype(BF16)
        send_dy.append(Exchange("ctx", n, rows(sdy, h), rows(rdy, h), rdy.at[h, :most], *pair()))
        send_dy[h].start()
        rdy[h, own, :] = sdy[h, own, :]

    if late is not None:
        gather_late = Exchange("exp", m, lambda p: xg.at[mine], lambda s: xg.at[s], xg.at[:m - 1], *pair())
    dispatch_cot(0)
    if late is not None:
        launch_x.arrive()
        gather_late.start()
    for h in range(1, nc):
        dispatch_cot(h)
    share.arrive()
    total = jnp.sum(side[...], axis=0)[:1, :tokens]
    sc[...] = column(lax.rsqrt(total / width + EPS))
    send_x = []
    for h in direct:
        gather_mixed[h].arrive()
        for k, part in enumerate(spread(pt[...], [mx[h, k] for k in range(m)])):
            sx[h, :, spans(h, k)] = part.astype(BF16)
        send_x.append(Exchange("ctx", n, rows(sx, h), rows(xa, h), xa.at[h, :most], *pair()))
        send_x[h].start()
        xa[h, own, :] = sx[h, own, :]

    tile = min(256, inner)
    tiles = [slice(f, f + tile) for f in range(0, inner, tile)]
    step = 32

    def raw(k, h, at):
        return (xg[k, at, :] if h == late else xa[h, at, spans(h, k)]).astype(F32)

    def weigh(h):
        for r in range(0, slots, step):
            at = slice(r, r + step)
            acc = jnp.zeros((step, cw), F32)
            for k in range(m):
                part = raw(k, h, at)
                acc = acc + part * part
                gained[h, at, spans(h, k)] = (part * gain_of(k, h)).astype(BF16)
            total = jnp.broadcast_to(jnp.sum(acc, axis=1, keepdims=True), (step, 128))
            unit[at] = total if h == first else unit[at] + total

    def chan_rows(ref, h, cols):
        if nc == 1:
            return ref[:, cols]
        return jnp.concatenate(
            [ref[k * chans + h * cw : k * chans + (h + 1) * cw, cols] for k in range(m)], axis=0
        )

    def project(h, f):
        for ref, w in ((ga, wg), (ua, wu)):
            part = dot(gained[h], chan_rows(w, h, f))
            ref[:, f] = part if h == first else ref[:, f] + part

    weights[0].wait()
    weights[1].wait()
    weights[2].wait()
    first = direct[0] if late is None else late
    if late is not None:
        gather_late.arrive()
        weigh(late)
        for f in tiles:
            project(late, f)
    for h in range(nc):
        send_dy[h].arrive()
    d_y = natural(rdy, 0, width)
    for f in tiles:
        dh[:, f] = dot(d_y, wd[f, :], LAST)
    for h in direct:
        send_x[h].arrive()
        weigh(h)
    unit[...] = lax.rsqrt(unit[...] / width + EPS)
    for f in tiles:
        for h in direct:
            project(h, f)
        for r in range(0, slots, step):
            at = slice(r, r + step)
            each = jnp.concatenate([unit[at]] * (tile // 128), axis=1)
            g, u, d = ga[at, f] * each, ua[at, f] * each, dh[at, f]
            sigma = jax.nn.sigmoid(g)
            swish = g * sigma
            hid[at, f] = (swish * u).astype(BF16)
            dg[at, f] = (d * u * sigma * (1.0 + g * (1.0 - sigma))).astype(BF16)
            du[at, f] = (d * swish).astype(BF16)
    group = max(1, min(m, 256 // cw))
    def row_grads(h):
        for k in range(0, m, group):
            if nc == 1:
                at = slice(k * cw, (k + group) * cw)
                w1, w2 = wg[at, :], wu[at, :]
            else:
                w1, w2 = [
                    jnp.concatenate(
                        [w[j * chans + h * cw : j * chans + (h + 1) * cw, :] for j in range(k, k + group)], axis=0
                    )
                    for w in (wg, wu)
                ]
            yield k, dot(dg[...], w1, LAST) + dot(du[...], w2, LAST)

    send_dx, send_y = [], []
    if late is not None:
        inner_q = jnp.zeros((slots, cw), F32)
        for k, part in row_grads(late):
            for j in range(k, k + group):
                piece = part[:, (j - k) * cw : (j - k + 1) * cw]
                sl[j] = piece.astype(BF16)
                inner_q = inner_q + piece * raw(j, late, slice(None)) * gain_of(j, late)
        reduce_late = Exchange("exp", m, lambda p: sl.at[p], lambda s: rl.at[s], rl.at[:m - 1], *pair())
        rl[mine] = sl[mine]
        inner_q = jnp.sum(inner_q, axis=1, keepdims=True)
        high = inner_q.astype(BF16).astype(F32)
        lane = lax.broadcasted_iota(jnp.int32, (slots, 128), 1)
        sdx[0, :, span_all:] = jnp.where(
            lane == 0, high, jnp.where(lane == 1, inner_q - high, 0.0)
        ).astype(BF16)
    def act_dx():
        for h in direct:
            for k, part in row_grads(h):
                sdx[h, :, k * cw : (k + group) * cw] = part.astype(BF16)
            send_dx.append(Exchange("ctx", n, rows(sdx, h), rows(bdx, h), bdx.at[h, :most], *pair()))
            send_dx[h].start()
            bdx[h, own, :] = sdx[h, own, :]
    def act_y(h):
        for k in range(0, m, group):
            if nc == 1:
                w = wd[:, k * cw : (k + group) * cw]
            else:
                w = jnp.concatenate(
                    [wd[:, j * chans + h * cw : j * chans + (h + 1) * cw] for j in range(k, k + group)], axis=1
                )
            sy[h, :, k * cw : (k + group) * cw] = dot(hid[...], w).astype(BF16)
        send_y.append(Exchange("ctx", n, rows(sy, h), rows(by, h), by.at[h, :most], *pair()))
        send_y[h].start()
        by[h, own, :] = sy[h, own, :]

    def act_grads(part):
        if part == 0:
            for f in tiles:
                gwd_ref[f, :] = dot(hid[:, f], natural(rdy, 0, width), FIRST).astype(BF16)
        if part == 1:
            for r in range(0, slots, step):
                at = slice(r, r + step)
                for k in range(m):
                    for h in range(nc):
                        lo = k * chans + h * cw
                        normed = raw(k, h, at) * gain_of(k, h) * unit[at, :cw]
                        rx[at, lo : lo + cw] = normed.astype(BF16)
            for lo in range(0, width, 256):
                part = rx[:, lo : lo + 256]
                gwg_ref[lo : lo + 256, :] = dot(part, dg[...], FIRST).astype(BF16)
                gwu_ref[lo : lo + 256, :] = dot(part, du[...], FIRST).astype(BF16)

    act_dx()
    if late is not None:
        reduce_late.start()
    act_y(0)
    act_grads(0)
    act_grads(1)
    for h in range(1, nc):
        act_y(h)

    sum_dx, sum_y = [], []
    weighted = jnp.zeros((tokens, cw), F32)
    sum_norm = Exchange("exp", m, lambda p: norm.at[mine], lambda s: norm.at[s], norm.at[:m - 1], *pair())
    for h in direct:
        send_dx[h].arrive()
        full = dot(pb[...], bdx[h])
        if h == 0 and late is not None:
            late_q = full[:, span_all : span_all + 1] + full[:, span_all + 1 : span_all + 2]
        for k in range(m):
            part = full[:, spans(h, k)]
            zdx[h, k] = part.astype(BF16)
            weighted = weighted + part * mx[h, k].astype(F32) * gain_of(k, h)
        if h == direct[-1]:
            total_q = jnp.sum(weighted, axis=1, keepdims=True)
            if late is not None:
                total_q = total_q + late_q
            norm[mine] = jnp.broadcast_to(turn_row(total_q), norm.shape[1:])
            sum_norm.start()
        sum_dx.append(
            Exchange("exp", m, lambda p, h=h: zdx.at[h, p], lambda s, h=h: rdx.at[h, s], rdx.at[h, :m - 1], *pair())
        )
        sum_dx[h].start()
        rdx[h, mine] = zdx[h, mine]
    def combine(h, d0, d1):
        send_y[h].arrive()
        y0, y1 = dot(p0s[...], by[h]), dot(p1s[...], by[h])
        for k in range(m):
            a, b = y0[:, spans(h, k)], y1[:, spans(h, k)]
            zy[h, k] = (a * gc[0, :, :cw] + b * gc[1, :, :cw]).astype(BF16)
            cot = cots[h, k].astype(F32)
            d0, d1 = d0 + a * cot, d1 + b * cot
        sum_y.append(
            Exchange("exp", m, lambda p, h=h: zy.at[h, p], lambda s, h=h: ry.at[h, s], ry.at[h, :m - 1], *pair())
        )
        sum_y[h].start()
        ry[h, mine] = zy[h, mine]
        return d0, d1

    d0 = jnp.zeros((tokens, cw), F32)
    d1 = jnp.zeros((tokens, cw), F32)
    if late is not None:
        reduce_late.arrive()
        ol[...] = jnp.sum(rl[...].astype(F32), axis=0).astype(BF16)
        send_late = Exchange("ctx", n, rows(ol), rows(bl), bl.at[:most], *pair())
        send_late.start()
        bl[own, :] = ol[own, :]

    for h in range(nc):
        d0, d1 = combine(h, d0, d1)
    for h in direct:
        sum_dx[h].arrive()
    sum_norm.arrive()
    if late is not None:
        send_late.arrive()
    q = column(jnp.sum(norm[...], axis=0)[:1])
    scale = sc[...]
    pull = q * scale * scale * scale / width
    for h in range(nc):
        lanes = slice(h * cw, (h + 1) * cw)
        dn = dot(pb[...], bl[...]) if h == late else jnp.sum(rdx[h].astype(F32), axis=0)
        mixed = mx[h, mine].astype(F32)
        dm = cots[h, mine].astype(F32) + gain_row[:, lanes] * dn * scale[:, :cw] - mixed * pull[:, :cw]
        dmp[EDGE : EDGE + tokens, lanes] = dm
        de[0, :, lanes] = dm[:EDGE].astype(BF16)
        de[1, :, lanes] = dm[tokens - EDGE :].astype(BF16)
        tp[me, taps : taps + 1, lanes] = jnp.sum(
            dn * mixed * scale[:, :cw], axis=0, keepdims=True
        ).astype(BF16)
    halo_d = Halo(n, de, dl, dr, hs2)
    halo_d.start()
    for h in range(nc):
        lanes = slice(h * cw, (h + 1) * cw)
        dm = dmp[EDGE : EDGE + tokens, lanes]
        for j in range(taps):
            o = base + j
            b = o % 8
            term = jnp.sum(dm * xs[b, o - b : o - b + tokens, lanes], axis=0, keepdims=True)
            tp[me, j : j + 1, lanes] = term.astype(BF16)
    sum_taps = Exchange("ctx", n, lambda p: tp.at[me], lambda s: tp.at[s], tp.at[:n - 1], *pair())
    sum_taps.start()
    dots[mine, 0:1, :] = turn_row(jnp.sum(d0, axis=1, keepdims=True))
    dots[mine, 1:2, :] = turn_row(jnp.sum(d1, axis=1, keepdims=True))
    sum_dots = Exchange("exp", m, lambda p: dots.at[mine], lambda s: dots.at[s], dots.at[:m - 1], *pair())
    sum_dots.start()

    halo_d.arrive()
    dmp[:EDGE, :] = dl[...].astype(F32)
    dmp[EDGE + tokens :, :] = dr[...].astype(F32)
    low = EDGE + taps // 2 - (taps - 1)
    for h in range(nc):
        lanes = slice(h * cw, (h + 1) * cw)
        block = dmp[:, lanes]
        acc = dmp[EDGE : EDGE + tokens, lanes]
        for b, moved, offs in windows(block, low, taps):
            for o in offs:
                j = EDGE + taps // 2 - o
                acc = acc + tap_s[j : j + 1, lanes] * moved[o - b : o - b + tokens]
        gin_ref[lanes, :] = jnp.transpose(acc).astype(BF16)
    sum_taps.arrive()
    grads = jnp.sum(tp[...].astype(F32), axis=0)
    tapo_ref[...] = grads[:taps]
    gaino_ref[...] = grads[taps : taps + 1]
    for h in range(nc):
        sum_y[h].arrive()
        out = mx[h, mine].astype(F32) + jnp.sum(ry[h].astype(F32), axis=0)
        lo_ref[h * cw : (h + 1) * cw, :] = jnp.transpose(out).astype(BF16)
    sum_dots.arrive()
    gateo_ref[...] = jnp.sum(dots[...], axis=0)[:2]
    singles = [halo, halo_d, share, sum_norm, sum_dots, sum_taps]
    if late is not None:
        singles += [reduce_late, send_late, launch_x, gather_late]
    for group in (singles, gather_cot, gather_mixed, send_x, send_dy, send_dx, send_y, sum_dx, sum_y):
        for done in group:
            done.sent()


def finish(*refs):
    count = (len(refs) - 1) // 2
    sem = refs[-1]
    copies = [
        pltpu.make_async_copy(refs[i], refs[count + i], sem.at[i]) for i in range(count)
    ]
    for copy in copies:
        copy.start()
    for copy in copies:
        copy.wait()


def local(inputs, conv_taps, norm_gain, routes, gate_probs, w_gate, w_up, w_down, grad_out):
    chans, tokens = inputs.shape
    taps = conv_taps.shape[1]
    width, inner = w_gate.shape[1:]
    n, m = lax.axis_size("ctx"), lax.axis_size("exp")
    cap = max(tokens // 8, (2 * tokens + n - 1) // n)
    slots = n * cap
    pad = -(-(taps + 1) // 16) * 16
    nc = 2 if chans % 256 == 0 else 1
    cw = chans // nc
    vmem = pl.BlockSpec(memory_space=pltpu.VMEM)
    hbm = pl.BlockSpec(memory_space=pltpu.HBM)
    shape = jax.ShapeDtypeStruct
    dma = pltpu.SemaphoreType.DMA
    V = pltpu.VMEM
    outs = (
        shape((chans, tokens), BF16),
        shape((chans, tokens), BF16),
        shape((taps, chans), F32),
        shape((1, chans), F32),
        shape((2, tokens), F32),
        shape((width, inner), BF16),
        shape((width, inner), BF16),
        shape((inner, width), BF16),
    )
    straight = nc - 1 if nc > 1 else 1
    extra = nc > 1
    big = V((nc, slots, m * cw), BF16)
    part = V((nc, slots, m * cw), BF16)
    plus = V((straight, slots, m * cw + 128 * extra), BF16)
    operands = [
        pltpu.with_memory_space_constraint(a, pltpu.HBM)
        for a in (
            inputs, conv_taps.T, norm_gain, routes.T, gate_probs.T, grad_out, w_gate, w_up, w_down
        )
    ]
    results = pl.pallas_call(
        functools.partial(layer, n, m, taps, cap, nc),
        out_shape=outs,
        in_specs=[hbm] * 9,
        out_specs=(vmem,) * 8,
        scratch_shapes=[
            V((chans, tokens), BF16), V((taps, chans), F32), V((chans,), BF16),
            V((2, tokens), jnp.int32), V((2, tokens), F32), V((chans, tokens), BF16),
            V((width, inner), BF16), V((width, inner), BF16), V((inner, width), BF16),
            V((tokens + 2 * EDGE, chans), F32), V((8, tokens + 24, chans), F32),
            V((2, EDGE, chans), BF16), V((EDGE, chans), BF16), V((EDGE, chans), BF16),
            V((nc, m, tokens, cw), BF16), V((nc, m, tokens, cw), BF16),
            V((m, 8, max(tokens, cw)), F32),
            V((slots, tokens), BF16), V((tokens, slots), BF16), V((tokens, slots), BF16),
            V((tokens, slots), BF16),
            V((slots, 128), F32), V((2, tokens, 128), F32), V((tokens, 128), F32),
            big, part, big, V((slots, width), BF16), V((slots, cw), BF16), part, V((m, slots, cw), BF16), big, V((slots, 128), F32),
            V((slots, inner), F32), V((slots, inner), F32), V((slots, inner), F32),
            V((slots, inner), BF16), V((slots, inner), BF16), V((slots, inner), BF16),
            plus, big, plus, big,
            V((m, slots, cw), BF16), V((m, slots, cw), BF16), V((slots, cw), BF16), V((slots, cw), BF16),
            V((nc, m, tokens, cw), BF16), V((nc, m, tokens, cw), BF16),
            V((nc, m, tokens, cw), BF16), V((nc, m, tokens, cw), BF16),
            V((m, 8, tokens), F32), V((m, 8, tokens), F32),
            V((tokens + 2 * EDGE, chans), F32),
            V((2, EDGE, chans), BF16), V((EDGE, chans), BF16), V((EDGE, chans), BF16),
            V((n, pad, chans), BF16),
            dma((9,)), dma((4,)), dma((4,)),
            dma((42,)),
        ],
        compiler_params=pltpu.CompilerParams(
            collective_id=0, has_side_effects=True, vmem_limit_bytes=36 << 20
        ),
        cost_estimate=pl.CostEstimate(
            flops=18 * slots * width * inner, bytes_accessed=12 * width * inner, transcendentals=slots * inner
        ),
        name="layer",
    )(*operands)
    results = pl.pallas_call(
        finish,
        out_shape=outs,
        in_specs=[vmem] * 8,
        out_specs=(hbm,) * 8,
        scratch_shapes=[dma((8,))],
        compiler_params=pltpu.CompilerParams(vmem_limit_bytes=16 << 20),
        name="finish",
    )(*results)
    layer_out, grad_in, grad_taps, grad_gain, grad_gates, grad_gate, grad_up, grad_down = results
    return (
        layer_out,
        grad_in,
        grad_taps.T,
        grad_gain[0],
        grad_gates.T,
        grad_gate[None],
        grad_up[None],
        grad_down[None],
    )


def solution(mesh):
    return jax.shard_map(
        local,
        mesh=mesh,
        in_specs=(
            P("exp", "ctx"),
            P("exp", None),
            P("exp"),
            P("ctx", None),
            P("ctx", None),
            P("ctx", None, "exp"),
            P("ctx", None, "exp"),
            P("ctx", "exp", None),
            P("exp", "ctx"),
        ),
        out_specs=(
            P("exp", "ctx"),
            P("exp", "ctx"),
            P("exp", None),
            P("exp"),
            P("ctx", None),
            P("ctx", None, "exp"),
            P("ctx", None, "exp"),
            P("ctx", "exp", None),
        ),
        check_vma=False,
    )
```
